1024 devices in a mesh: dp: 64 (over x, z_lo), tensor: 16 (over y, z_hi, core).
Axes of the slice: x: 4, y: 4, z: 32 (z_hi: 2, z_lo: 16; z = z_hi * 16 + z_lo), core: 2. Of those that a mesh axis runs over, the one named last changes fastest.
Arguments:
- tokens: bfloat16 [16384, 4096], P(('dp', 'tensor')), may hold values from -24 to 24
- q_weight: bfloat16 [4096, 2048], P('dp', 'tensor'), may hold values from -3.90625 to 3.90625
- k_weight: bfloat16 [4096, 1024], P('dp', 'tensor'), may hold values from -0.125 to 0.125, as said below
- v_weight: bfloat16 [4096, 1024], P('dp', 'tensor'), may hold values from -0.09375 to 0.09375
- d_context: bfloat16 [16384, 2048], P('dp', 'tensor'), may hold values from -6 to 6
Outputs:
- context: bfloat16 [16384, 2048], P('dp', 'tensor')
- grad_tokens: bfloat16 [16384, 4096], P(('dp', 'tensor'))
- grad_q: float32 [4096, 2048], P('dp', 'tensor')
- grad_k: float32 [4096, 1024], P('dp', 'tensor')
- grad_v: float32 [4096, 1024], P('dp', 'tensor')
The draws below stay inside these ranges and needn't reach their ends.
Inputs may be any that keep to these rules, and one draw needn't show every extreme that they name: k_weight has independent entries.
All inputs are finite; a program needn't handle non-finite values.
Results may differ from the reference program's by a relative error of at most 0.02.
Values may be sent and summed in bfloat16 or wider, within the bound.
No kernel may reach another device: no remote copies, remote signals or barrier semaphores. Data moves between devices by JAX's collectives and lax.ppermute only.
A program may use at most 32 MiB of HBM per device.

```python
import math
import jax
import jax.numpy as jnp
from jax import lax

D = 4096
HEAD = 128
SEQ = 16
TOKENS = 16384
Q_HEADS = 16
KV_HEADS = 8
N_TENSOR = 16


def draw_q_weight(key, part):
    key = jax.random.fold_in(key, 5)
    private = jax.random.truncated_normal(jax.random.fold_in(key, 1), -6.0, 6.0, (D, Q_HEADS, HEAD), jnp.float32)
    combined = private
    return (combined / math.sqrt(D)).reshape(D, Q_HEADS * HEAD).astype(jnp.bfloat16)


def draw_k_weight(key, part):
    key = jax.random.fold_in(key, 7)
    private = jax.random.truncated_normal(jax.random.fold_in(key, 1), -6.0, 6.0, (D, KV_HEADS, HEAD), jnp.float32)
    combined = private
    return (combined / math.sqrt(D)).reshape(D, KV_HEADS * HEAD).astype(jnp.bfloat16)


def spiked(values, rng, source, target, blocks, factor):
    owner, partner = [(jnp.arange(values.shape[axis_at]) // (values.shape[axis_at] // blocks)).reshape([-1 if axis == axis_at else 1 for axis in range(values.ndim)]) for axis_at in (source, target)]
    chosen = jax.random.permutation(rng, blocks)[partner]
    strong = (owner == chosen) | (owner == (partner + blocks // 2) % blocks)
    return jnp.where(strong, factor * values, values)


def levels(own_key, dims, split, smallest, high):
    def one(dim, shards_of):
        heights = jax.random.uniform(jax.random.fold_in(jax.random.fold_in(own_key, 6), dim), (shards_of,), jnp.float32, smallest / len(split), high / len(split))
        return jnp.repeat(jnp.exp(heights), dims[dim] // shards_of).reshape((-1,) + (1,) * (len(dims) - dim - 1))

    loudness = one(*split[0])
    for cut in split[1:]:
        loudness = loudness * one(*cut)
    return loudness


def bell_draw(key, extent, deviation, bound, cuts=(), dtype=jnp.bfloat16):
    factor_of = levels(key, extent, cuts, -0.22, 0.18) if cuts else 1.0
    drawn = jax.random.normal(key, extent, jnp.float32) * deviation * factor_of
    return jnp.minimum(jnp.maximum(drawn, -bound), bound).astype(dtype)


def bell_draw_with(stream_key, dims, spread, limit, pieces, heavy, kind=jnp.bfloat16):
    entries = spread * jax.random.normal(stream_key, dims, jnp.float32)
    if pieces:
        entries = entries * levels(stream_key, dims, pieces, -0.22, 0.18)
    return jnp.clip(spiked(entries, jax.random.fold_in(stream_key, 3), *heavy), -limit, limit).astype(kind)


def setup_inputs(seed: int = 0) -> dict:
    keys = jax.random.split(jax.random.key(seed), 6)
    return {
        "tokens": bell_draw_with(keys[0], (TOKENS, D), 1.0, 24.0, ((0, 1024),), (0, 1, 1024, 6.0)),
        "q_weight": draw_q_weight(jax.random.fold_in(keys[5], 71), 0),
        "k_weight": draw_k_weight(jax.random.fold_in(keys[5], 71), 0),
        "v_weight": bell_draw(keys[3], (D, KV_HEADS * HEAD), D ** -0.5, 0.09375, ((0, 64), (1, 16))),
        "d_context": bell_draw(keys[4], (TOKENS, Q_HEADS * HEAD), 1.0, 6.0, ((0, 64), (1, 16))),
    }


def rope_tables(count):
    position = (jnp.arange(count) % SEQ).astype(jnp.float32)
    exponent = jnp.arange(HEAD // 2).astype(jnp.float32) * (2.0 / HEAD)
    inverse = jnp.exp(-exponent * jnp.log(500000.0))
    angles = position[:, None] * inverse[None, :]
    return (jnp.cos(angles)[:, None, :], jnp.sin(angles)[:, None, :])

def rotate(values, cosine, sine):
    half_size = values.shape[-1] // 2
    first = values[..., :half_size]
    second = values[..., half_size:]
    return jnp.concatenate([first * cosine - second * sine, second * cosine + first * sine], axis=-1)

def unrotate(grads, cosine, sine):
    half_size = grads.shape[-1] // 2
    first = grads[..., :half_size]
    second = grads[..., half_size:]
    return jnp.concatenate([first * cosine + second * sine, second * cosine - first * sine], axis=-1)

def reference(tokens, q_weight, k_weight, v_weight, d_context):
    scale = 1.0 / math.sqrt(HEAD)
    inputs = tokens.astype(jnp.float32)
    inv_rms = lax.rsqrt(lax.optimization_barrier(jnp.mean(inputs * inputs, axis=-1, keepdims=True)) + 1e-05)
    normed = (inputs * inv_rms).astype(jnp.bfloat16)
    cosine, sine = rope_tables(TOKENS)
    q_raw = jnp.dot(normed, q_weight, preferred_element_type=jnp.float32).reshape(TOKENS, Q_HEADS, HEAD)
    query = rotate(q_raw, cosine, sine).astype(jnp.bfloat16)
    key_raw = jnp.dot(normed, k_weight, preferred_element_type=jnp.float32).astype(jnp.bfloat16)
    key_rot = rotate(key_raw.astype(jnp.float32).reshape(TOKENS, KV_HEADS, HEAD), cosine, sine).astype(jnp.bfloat16)
    value = jnp.dot(normed, v_weight, preferred_element_type=jnp.float32).astype(jnp.bfloat16)
    value = value.reshape(TOKENS, KV_HEADS, HEAD)
    batches = TOKENS // SEQ
    query_b = query.reshape(batches, SEQ, Q_HEADS, HEAD).astype(jnp.float32)
    key_b = jnp.repeat(key_rot, 2, axis=1).reshape(batches, SEQ, Q_HEADS, HEAD).astype(jnp.float32)
    value_b = jnp.repeat(value, 2, axis=1).reshape(batches, SEQ, Q_HEADS, HEAD).astype(jnp.float32)
    places = jnp.arange(SEQ)
    allowed = places[None, :] <= places[:, None]
    scores = jnp.einsum('bihd,bjhd->bhij', query_b, key_b) * scale
    masked = jnp.where(allowed, scores, -1e+30)
    largest = lax.optimization_barrier(jnp.max(masked, axis=-1, keepdims=True))
    expd = jnp.exp(masked - largest)
    probs = expd / lax.optimization_barrier(jnp.sum(expd, axis=-1, keepdims=True))
    probs_b = probs.astype(jnp.bfloat16).astype(jnp.float32)
    context = jnp.einsum('bhij,bjhd->bihd', probs_b, value_b).astype(jnp.bfloat16)
    context = context.reshape(TOKENS, Q_HEADS * HEAD)
    grad_out = d_context.astype(jnp.float32).reshape(batches, SEQ, Q_HEADS, HEAD)
    d_probs = jnp.einsum('bihd,bjhd->bhij', grad_out, value_b)
    d_scores = probs * (d_probs - lax.optimization_barrier(jnp.sum(probs * d_probs, axis=-1, keepdims=True))) * scale
    d_scores = d_scores.astype(jnp.bfloat16).astype(jnp.float32)
    value_term = jnp.einsum('bhij,bihd->bjhd', probs_b, grad_out).reshape(TOKENS, Q_HEADS, HEAD)
    dq_rot = jnp.einsum('bhij,bjhd->bihd', d_scores, key_b).reshape(TOKENS, Q_HEADS, HEAD)
    dk_rot = jnp.einsum('bhij,bihd->bjhd', d_scores, query_b).reshape(TOKENS, Q_HEADS, HEAD)
    d_query = unrotate(dq_rot, cosine, sine).astype(jnp.bfloat16).reshape(TOKENS, Q_HEADS * HEAD)
    key_term = unrotate(dk_rot, cosine, sine).astype(jnp.bfloat16).astype(jnp.float32)
    value_term = value_term.astype(jnp.bfloat16).astype(jnp.float32)
    d_key = key_term.reshape(TOKENS, KV_HEADS, 2, HEAD).sum(axis=2).astype(jnp.bfloat16)
    d_value = value_term.reshape(TOKENS, KV_HEADS, 2, HEAD).sum(axis=2).astype(jnp.bfloat16)
    d_key = d_key.reshape(TOKENS, KV_HEADS * HEAD)
    d_value = d_value.reshape(TOKENS, KV_HEADS * HEAD)
    grad_q = jnp.dot(normed.T, d_query, preferred_element_type=jnp.float32)
    grad_k = jnp.dot(normed.T, d_key, preferred_element_type=jnp.float32)
    grad_v = jnp.dot(normed.T, d_value, preferred_element_type=jnp.float32)
    half_size = HEAD // 2
    d_normed = jnp.zeros((TOKENS, D), jnp.float32)
    for group in range(N_TENSOR):
        q_cols = slice(group * HEAD, (group + 1) * HEAD)
        k_cols = slice(group * half_size, (group + 1) * half_size)
        part = jnp.dot(d_query[:, q_cols], q_weight[:, q_cols].T, preferred_element_type=jnp.float32)
        part = part + jnp.dot(d_key[:, k_cols], k_weight[:, k_cols].T, preferred_element_type=jnp.float32)
        part = part + jnp.dot(d_value[:, k_cols], v_weight[:, k_cols].T, preferred_element_type=jnp.float32)
        d_normed = d_normed + part.astype(jnp.bfloat16).astype(jnp.float32)
    cubed = inv_rms * inv_rms * inv_rms
    grad_tokens = inv_rms * d_normed - inputs * cubed * lax.optimization_barrier(jnp.mean(inputs * d_normed, axis=-1, keepdims=True))
    return (context, grad_tokens.astype(jnp.bfloat16), grad_q, grad_k, grad_v)
```

```python
import functools
import math

import jax
import jax.numpy as jnp
import numpy as np
from jax import lax
from jax.experimental import pallas as pl
from jax.experimental.pallas import tpu as pltpu
from jax.sharding import Mesh
from jax.sharding import PartitionSpec as P

SEQ = 16
SHIFTS = (0, -1, 1, 2)
VMEM_LIMIT = 40 * 1024 * 1024

AXES = ("x", "zl", "y", "zh", "co")
SIZES = (4, 16, 4, 2, 2)
DP = ("x", "zl")
TENSOR = ("y", "zh", "co")


def flipped(value, axis, mask):
    size = lax.axis_size(axis)
    return lax.ppermute(value, axis, [(s, s ^ mask) for s in range(size)])


def shifted(value, axis, step):
    size = lax.axis_size(axis)
    return lax.ppermute(value, axis, [(s, (s + step) % size) for s in range(size)])


def z_masks():
    masks = []
    mask = SIZES[1] // 2
    while mask:
        masks.append(mask)
        mask //= 2
    return masks


def z_offset(place):
    return sum(m for bit, m in enumerate(z_masks()) if place >> bit & 1)


def ring_gather(block, axis):
    half = block.shape[0] // 2
    left = shifted(block, axis, 1)
    right = shifted(block, axis, -1)
    far_a = shifted(left[:half], axis, 1)
    far_b = shifted(right[half:], axis, -1)
    return left, right, far_a, far_b


def added(*terms):
    total = terms[0].astype(jnp.float32)
    for term in terms[1:]:
        total = total + term.astype(jnp.float32)
    return total


def ring_scatter(own, left, right, far_a, far_b, axis):
    half = own.shape[0] // 2
    got_a = shifted(far_a, axis, 1)
    got_b = shifted(far_b, axis, -1)
    to_right = jnp.concatenate(
        [added(right[:half], got_a).astype(jnp.bfloat16), right[half:]], axis=0
    )
    to_left = jnp.concatenate(
        [left[:half], added(left[half:], got_b).astype(jnp.bfloat16)], axis=0
    )
    from_left = shifted(to_right, axis, 1)
    from_right = shifted(to_left, axis, -1)
    return added(own, from_left, from_right)


def rope_tables(rows, head_size):
    position = (np.arange(rows) % SEQ).astype(np.float32)
    exponent = np.arange(head_size // 2).astype(np.float32) * np.float32(2.0 / head_size)
    inverse = np.exp(-exponent * np.log(np.float32(500000.0)))
    angles = position[:, None] * inverse[None, :]
    cosine, sine = np.cos(angles), np.sin(angles)
    return (
        np.concatenate([cosine, cosine], axis=1).astype(np.float32),
        np.concatenate([-sine, sine], axis=1).astype(np.float32),
    )


def half_roll(value):
    return pltpu.roll(value, value.shape[-1] // 2, 1)


def sequence_at(place, ids):
    co, yq, zh = place // 8, place // 2 % 4, place % 2
    y = (ids[2] + SHIFTS[yq] + 4) % 4
    return y * 4 + (ids[3] ^ zh) * 2 + (ids[4] ^ co)


def project_kernel(zs, ids, t0, t1, w_own, w_left, w_right, w_fa, w_fb, cos, sin, w_out, q_out, kv_out):
    rows = w_own.shape[0]
    unit = rows // zs
    pieces = ((w_own, 0, 0, zs), (w_left, 1, 0, zs), (w_right, 2, 0, zs), (w_fa, 3, 0, zs // 2), (w_fb, 3, zs // 2, zs))
    for ref, ring, first, last in pieces:
        block = (ids[0] + SHIFTS[ring] + 4) % 4
        for place in range(first, last):
            z = ids[1] ^ z_offset(place)
            at = pl.multiple_of(block * rows + z * unit, unit)
            w_out[pl.ds(at, unit), :] = ref[(place - first) * unit : (place - first + 1) * unit, :]
    totals = []
    for ref in (t0, t1):
        total = None
        for k in range(4):
            cut = slice(k * rows, (k + 1) * rows)
            term = jnp.dot(ref[:, cut], w_out[cut, :], preferred_element_type=jnp.float32)
            total = term if total is None else total + term
        totals.append(total)
    projected = jnp.concatenate(totals, axis=0)
    head = projected.shape[1] // 2
    query = projected[:, :head]
    q_out[...] = (query * cos[...] + half_roll(query) * sin[...]).astype(jnp.bfloat16)
    kv_out[...] = projected[:, head:].astype(jnp.bfloat16)


def attend_kernel(ids, q_ref, mine_ref, other_ref, d_ctx_ref, cos, sin, ctx_out, dq_out, keep_out, send_out, d_ctx, ctx):
    rows, head = q_ref.shape
    half = rows // 2
    scale = 1.0 / math.sqrt(head)
    is_first = ids[4] == 0
    low = lax.broadcasted_iota(jnp.int32, (rows, head), 1) < head // 2
    mine = mine_ref[...].astype(jnp.float32)
    other = jnp.concatenate([other_ref[half:, :], other_ref[:half, :]], axis=0).astype(jnp.float32)
    a = jnp.where(is_first, mine, other)
    b = jnp.where(is_first, other, mine)
    key_raw = jnp.where(low, a, half_roll(b))
    value = jnp.where(low, half_roll(a), b).astype(jnp.bfloat16)
    key = (key_raw * cos[...] + half_roll(key_raw) * sin[...]).astype(jnp.bfloat16)
    query = q_ref[...]
    for place in range(rows // SEQ):
        at = pl.multiple_of(sequence_at(place, ids) * SEQ, SEQ)
        d_ctx[place * SEQ : (place + 1) * SEQ, :] = d_ctx_ref[pl.ds(at, SEQ), :]
    grad_out = d_ctx[...]
    row = lax.broadcasted_iota(jnp.int32, (rows, rows), 0)
    col = lax.broadcasted_iota(jnp.int32, (rows, rows), 1)
    allowed = (row // SEQ == col // SEQ) & (col <= row)
    last = (((1,), (1,)), ((), ()))
    first = (((0,), (0,)), ((), ()))
    dot = functools.partial(lax.dot_general, preferred_element_type=jnp.float32)
    scores = dot(query, key, last) * scale
    masked = jnp.where(allowed, scores, -1e30)
    expd = jnp.exp(masked - jnp.max(masked, axis=-1, keepdims=True))
    probs = expd / jnp.sum(expd, axis=-1, keepdims=True)
    probs_b = probs.astype(jnp.bfloat16)
    ctx[...] = jnp.dot(probs_b, value, preferred_element_type=jnp.float32).astype(jnp.bfloat16)
    for place in range(rows // SEQ):
        at = pl.multiple_of(sequence_at(place, ids) * SEQ, SEQ)
        ctx_out[pl.ds(at, SEQ), :] = ctx[place * SEQ : (place + 1) * SEQ, :]
    d_probs = dot(grad_out, value, last)
    d_scores = probs * (d_probs - jnp.sum(probs * d_probs, axis=-1, keepdims=True)) * scale
    d_scores = d_scores.astype(jnp.bfloat16)
    value_term = dot(probs_b, grad_out, first)
    dq_rot = jnp.dot(d_scores, key, preferred_element_type=jnp.float32)
    dk_rot = dot(d_scores, query, first)
    dq_out[...] = (dq_rot * cos[...] - half_roll(dq_rot) * sin[...]).astype(jnp.bfloat16)
    key_term = dk_rot * cos[...] - half_roll(dk_rot) * sin[...]
    lows = jnp.where(low, key_term, half_roll(value_term))
    highs = jnp.where(low, half_roll(key_term), value_term)
    keep_out[...] = jnp.where(is_first, lows, highs).astype(jnp.bfloat16)
    send_out[...] = jnp.where(is_first, highs, lows).astype(jnp.bfloat16)


def joined_grads(dq_ref, keep_ref, got_ref):
    half = dq_ref.shape[0] // 2
    got = jnp.concatenate([got_ref[half:, :], got_ref[:half, :]], axis=0)
    d_kv = (keep_ref[...].astype(jnp.float32) + got.astype(jnp.float32)).astype(jnp.bfloat16)
    return jnp.concatenate([dq_ref[...], d_kv], axis=1)


def weight_grad_kernel(zs, ids, t0, t1, dq_ref, keep_ref, got_ref, own, left, right, far_a, far_b, dj_out, natural):
    joined = joined_grads(dq_ref, keep_ref, got_ref)
    dj_out[...] = joined
    half = joined.shape[0] // 2
    rows = own.shape[0]
    unit = rows // zs
    dims = (((0,), (0,)), ((), ()))
    pieces = ((far_a, far_b, 3), (left, None, 1), (right, None, 2), (own, None, 0))
    for ref, second, ring in pieces:
        block = (ids[0] + SHIFTS[ring] + 4) % 4
        cut = pl.ds(pl.multiple_of(block * rows, rows), rows)
        total = lax.dot_general(t0[:, cut], joined[:half], dims, preferred_element_type=jnp.float32)
        total += lax.dot_general(t1[:, cut], joined[half:], dims, preferred_element_type=jnp.float32)
        natural[...] = total.astype(jnp.bfloat16)
        for place in range(zs):
            at = pl.multiple_of((ids[1] ^ z_offset(place)) * unit, unit)
            target, where = ref, place
            if second is not None and place >= zs // 2:
                target, where = second, place - zs // 2
            target[where * unit : (where + 1) * unit, :] = natural[pl.ds(at, unit), :]


def token_grad_kernel(dj_ref, w_ref, mine_out, send_out):
    half, width = mine_out.shape
    step = width // 4
    dims = (((1,), (1,)), ((), ()))
    for ref, rows in ((send_out, slice(half, None)), (mine_out, slice(0, half))):
        for k in range(4):
            cut = slice(k * step, (k + 1) * step)
            ref[:, cut] = lax.dot_general(
                dj_ref[rows, :], w_ref[cut, :], dims, preferred_element_type=jnp.float32
            ).astype(jnp.bfloat16)


def call(kernel, out_shapes, *args, scratch=(), flops=0, moved=0):
    vmem = pl.BlockSpec(memory_space=pltpu.VMEM)
    smem = pl.BlockSpec(memory_space=pltpu.SMEM)
    return pl.pallas_call(
        kernel,
        out_shape=[jax.ShapeDtypeStruct(s, jnp.bfloat16) for s in out_shapes],
        in_specs=[smem if a.dtype == jnp.int32 else vmem for a in args],
        out_specs=[vmem] * len(out_shapes),
        scratch_shapes=[pltpu.VMEM(s, jnp.bfloat16) for s in scratch],
        compiler_params=pltpu.CompilerParams(vmem_limit_bytes=VMEM_LIMIT),
        cost_estimate=pl.CostEstimate(flops=flops, bytes_accessed=moved, transcendentals=0),
    )(*args)


def shards(tokens, q_weight, k_weight, v_weight, d_context):
    head = q_weight.shape[1]
    width = tokens.shape[1]
    zs = SIZES[1]
    ids = jnp.stack([lax.axis_index(a) for a in AXES]).astype(jnp.int32)

    weights = jnp.concatenate([q_weight, k_weight, v_weight], axis=1)
    for mask in z_masks():
        weights = jnp.concatenate([weights, flipped(weights, "zl", mask)], axis=0)
    w_pieces = (weights, *ring_gather(weights, "x"))

    inputs = tokens.astype(jnp.float32)
    inv_rms = lax.rsqrt(jnp.mean(inputs * inputs, axis=-1, keepdims=True) + 1e-05)
    normed = (inputs * inv_rms).astype(jnp.bfloat16)
    normed = jnp.concatenate([normed, flipped(normed, "zh", 1)], axis=0)
    t0 = jnp.concatenate([normed, *ring_gather(normed, "y")], axis=0)
    t1 = flipped(t0, "co", 1)

    half = t0.shape[0]
    rows = 2 * half
    cosine, sine = (jnp.asarray(t) for t in rope_tables(rows, head))
    product = 2 * rows * width * 2 * head
    w_natural, query, kv_mine = call(
        functools.partial(project_kernel, zs),
        [(width, 2 * head), (rows, head), (rows, head)],
        ids, t0, t1, *w_pieces, cosine, sine,
        flops=product, moved=6 * width * rows,
    )
    kv_other = flipped(kv_mine, "co", 1)
    context, d_query, keep, send = call(
        attend_kernel,
        [(rows, head)] * 4,
        ids, query, kv_mine, kv_other, d_context, cosine, sine,
        scratch=[(rows, head)] * 2,
        flops=14 * rows * rows * head, moved=24 * rows * head,
    )
    got = flipped(send, "co", 1)
    block = width // SIZES[0]
    *g_pieces, joined = call(
        functools.partial(weight_grad_kernel, zs),
        [(block, 2 * head)] * 3 + [(block // 2, 2 * head)] * 2 + [(rows, 2 * head)],
        ids, t0, t1, d_query, keep, got,
        scratch=[(block, 2 * head)],
        flops=product, moved=4 * width * rows,
    )
    p_mine, p_send = call(
        token_grad_kernel,
        [(half, width)] * 2,
        joined, w_natural,
        flops=product, moved=4 * width * rows,
    )

    grads = ring_scatter(*g_pieces, "x")
    for mask in reversed(z_masks()):
        cut = grads.shape[0] // 2
        grads = grads[:cut] + flipped(grads[cut:].astype(jnp.bfloat16), "zl", mask).astype(jnp.float32)

    part = added(p_mine, flipped(p_send, "co", 1)).astype(jnp.bfloat16)
    quarter = half // 4
    far = part[3 * quarter :]
    part = ring_scatter(
        part[:quarter], part[quarter : 2 * quarter], part[2 * quarter : 3 * quarter],
        far[: quarter // 2], far[quarter // 2 :], "y",
    )
    cut = part.shape[0] // 2
    d_normed = part[:cut] + flipped(part[cut:].astype(jnp.bfloat16), "zh", 1).astype(jnp.float32)
    cubed = inv_rms * inv_rms * inv_rms
    grad_tokens = inv_rms * d_normed - inputs * cubed * jnp.mean(
        inputs * d_normed, axis=-1, keepdims=True
    )
    quart = head + head // 2
    return (context, grad_tokens.astype(jnp.bfloat16), grads[:, :head], grads[:, head:quart], grads[:, quart:])


def solution(mesh):
    split = P(DP, TENSOR)
    rows = P(DP + TENSOR, None)
    return jax.shard_map(
        shards,
        mesh=Mesh(mesh.devices.reshape(SIZES), AXES),
        in_specs=(rows, split, split, split, split),
        out_specs=(split, rows, split, split, split),
        check_vma=False,
    )
```

```python
import functools
import math

import jax
import jax.numpy as jnp
import numpy as np
from jax import lax
from jax.experimental import pallas as pl
from jax.experimental.pallas import tpu as pltpu
from jax.sharding import Mesh
from jax.sharding import PartitionSpec as P

SEQ = 16
SHIFTS = (0, -1, 1, 2)
VMEM_LIMIT = 40 * 1024 * 1024

AXES = ("x", "zl", "y", "zh", "co")
SIZES = (4, 16, 4, 2, 2)
DP = ("x", "zl")
TENSOR = ("y", "zh", "co")


def flipped(value, axis, mask):
    size = lax.axis_size(axis)
    return lax.ppermute(value, axis, [(s, s ^ mask) for s in range(size)])


def shifted(value, axis, step):
    size = lax.axis_size(axis)
    return lax.ppermute(value, axis, [(s, (s + step) % size) for s in range(size)])


RADIX = 4


def z_offset(place):
    return place % RADIX * RADIX + place // RADIX


def spread(block, axis, step):
    return tuple(flipped(block, axis, k * step) for k in range(1, RADIX))


def collect(blocks, axis, step):
    return tuple(flipped(block, axis, k * step) for k, block in enumerate(blocks, 1))


def ring_gather(block, axis):
    return tuple(shifted(block, axis, -shift) for shift in SHIFTS[1:])


def added(*terms):
    total = terms[0].astype(jnp.float32)
    for term in terms[1:]:
        total = total + term.astype(jnp.float32)
    return total


def ring_scatter(blocks, axis):
    return (blocks[0], *(shifted(block, axis, shift) for block, shift in zip(blocks[1:], SHIFTS[1:])))


def rope_tables(rows, head_size):
    position = (np.arange(rows) % SEQ).astype(np.float32)
    exponent = np.arange(head_size // 2).astype(np.float32) * np.float32(2.0 / head_size)
    inverse = np.exp(-exponent * np.log(np.float32(500000.0)))
    angles = position[:, None] * inverse[None, :]
    cosine, sine = np.cos(angles), np.sin(angles)
    return (
        np.concatenate([cosine, cosine], axis=1).astype(np.float32),
        np.concatenate([-sine, sine], axis=1).astype(np.float32),
    )


def half_roll(value):
    return pltpu.roll(value, value.shape[-1] // 2, 1)


def sequence_at(place, ids):
    co, yq, zh = place // 8, place // 2 % 4, place % 2
    y = (ids[2] + SHIFTS[yq] + 4) % 4
    return y * 4 + (ids[3] ^ zh) * 2 + (ids[4] ^ co)


def norm_kernel(tokens, inv_out, normed_out):
    inputs = tokens[...].astype(jnp.float32)
    inv = lax.rsqrt(jnp.mean(inputs * inputs, axis=-1, keepdims=True) + 1e-05)
    inv_out[...] = jnp.broadcast_to(inv, inv_out.shape)
    normed_out[...] = (inputs * inv).astype(jnp.bfloat16)


def rows_kernel(first, *refs):
    *parts, out = refs[first:]
    count = parts[0].shape[0]
    for place, ref in enumerate(parts):
        out[place * count : (place + 1) * count, :] = ref[...]


def scatter_sum_kernel(first, terms, *refs):
    parts, outs = refs[first : first + terms], refs[first + terms :]
    count = outs[0].shape[0]
    for place, out in enumerate(outs):
        cut = slice(place * count, (place + 1) * count)
        out[...] = added(*(part[cut, :] for part in parts)).astype(out.dtype)


def weights_out_kernel(own, a, b, c, q_out, k_out, v_out):
    total = added(own[...], a[...], b[...], c[...])
    head, half = q_out.shape[1], k_out.shape[1]
    q_out[...] = total[:, :head]
    k_out[...] = total[:, head : head + half]
    v_out[...] = total[:, head + half :]


def tokens_out_kernel(tokens, inv_wide, kept, got, out):
    inputs = tokens[...].astype(jnp.float32)
    d_normed = kept[...] + got[...].astype(jnp.float32)
    inv = inv_wide[:, :1]
    mean = jnp.mean(inputs * d_normed, axis=-1, keepdims=True)
    out[...] = (inv * d_normed - inputs * (inv * inv * inv) * mean).astype(jnp.bfloat16)


def project_kernel(zs, ids, t0, t1, w_own, w_left, w_right, w_far, cos, sin, w_out, q_out, kv_out):
    rows = w_own.shape[0]
    unit = rows // zs
    for ring, ref in enumerate((w_own, w_left, w_right, w_far)):
        block = (ids[0] + SHIFTS[ring] + 4) % 4
        for place in range(zs):
            z = ids[1] ^ z_offset(place)
            at = pl.multiple_of(block * rows + z * unit, unit)
            w_out[pl.ds(at, unit), :] = ref[place * unit : (place + 1) * unit, :]
    totals = []
    for ref in (t0, t1):
        total = None
        for k in range(4):
            cut = slice(k * rows, (k + 1) * rows)
            term = jnp.dot(ref[:, cut], w_out[cut, :], preferred_element_type=jnp.float32)
            total = term if total is None else total + term
        totals.append(total)
    projected = jnp.concatenate(totals, axis=0)
    head = projected.shape[1] // 2
    query = projected[:, :head]
    q_out[...] = (query * cos[...] + half_roll(query) * sin[...]).astype(jnp.bfloat16)
    kv_out[...] = projected[:, head:].astype(jnp.bfloat16)


def attend_kernel(ids, q_ref, mine_ref, other_ref, d_ctx_ref, cos, sin, ctx_out, dq_out, keep_out, send_out, d_ctx, ctx):
    rows, head = q_ref.shape
    half = rows // 2
    scale = 1.0 / math.sqrt(head)
    is_first = ids[4] == 0
    low = lax.broadcasted_iota(jnp.int32, (rows, head), 1) < head // 2
    mine = mine_ref[...].astype(jnp.float32)
    other = jnp.concatenate([other_ref[half:, :], other_ref[:half, :]], axis=0).astype(jnp.float32)
    a = jnp.where(is_first, mine, other)
    b = jnp.where(is_first, other, mine)
    key_raw = jnp.where(low, a, half_roll(b))
    value = jnp.where(low, half_roll(a), b).astype(jnp.bfloat16)
    key = (key_raw * cos[...] + half_roll(key_raw) * sin[...]).astype(jnp.bfloat16)
    query = q_ref[...]
    for place in range(rows // SEQ):
        at = pl.multiple_of(sequence_at(place, ids) * SEQ, SEQ)
        d_ctx[place * SEQ : (place + 1) * SEQ, :] = d_ctx_ref[pl.ds(at, SEQ), :]
    grad_out = d_ctx[...]
    row = lax.broadcasted_iota(jnp.int32, (rows, rows), 0)
    col = lax.broadcasted_iota(jnp.int32, (rows, rows), 1)
    allowed = (row // SEQ == col // SEQ) & (col <= row)
    last = (((1,), (1,)), ((), ()))
    first = (((0,), (0,)), ((), ()))
    dot = functools.partial(lax.dot_general, preferred_element_type=jnp.float32)
    scores = dot(query, key, last) * scale
    masked = jnp.where(allowed, scores, -1e30)
    expd = jnp.exp(masked - jnp.max(masked, axis=-1, keepdims=True))
    probs = expd / jnp.sum(expd, axis=-1, keepdims=True)
    probs_b = probs.astype(jnp.bfloat16)
    ctx[...] = jnp.dot(probs_b, value, preferred_element_type=jnp.float32).astype(jnp.bfloat16)
    for place in range(rows // SEQ):
        at = pl.multiple_of(sequence_at(place, ids) * SEQ, SEQ)
        ctx_out[pl.ds(at, SEQ), :] = ctx[place * SEQ : (place + 1) * SEQ, :]
    d_probs = dot(grad_out, value, last)
    d_scores = probs * (d_probs - jnp.sum(probs * d_probs, axis=-1, keepdims=True)) * scale
    d_scores = d_scores.astype(jnp.bfloat16)
    value_term = dot(probs_b, grad_out, first)
    dq_rot = jnp.dot(d_scores, key, preferred_element_type=jnp.float32)
    dk_rot = dot(d_scores, query, first)
    dq_out[...] = (dq_rot * cos[...] - half_roll(dq_rot) * sin[...]).astype(jnp.bfloat16)
    key_term = dk_rot * cos[...] - half_roll(dk_rot) * sin[...]
    lows = jnp.where(low, key_term, half_roll(value_term))
    highs = jnp.where(low, half_roll(key_term), value_term)
    keep_out[...] = jnp.where(is_first, lows, highs).astype(jnp.bfloat16)
    send_out[...] = jnp.where(is_first, highs, lows).astype(jnp.bfloat16)


def joined_grads(dq_ref, keep_ref, got_ref):
    half = dq_ref.shape[0] // 2
    got = jnp.concatenate([got_ref[half:, :], got_ref[:half, :]], axis=0)
    d_kv = (keep_ref[...].astype(jnp.float32) + got.astype(jnp.float32)).astype(jnp.bfloat16)
    return jnp.concatenate([dq_ref[...], d_kv], axis=1)


def weight_grad_kernel(zs, ids, t0, t1, dj_ref, own, left, right, far, natural):
    half = dj_ref.shape[0] // 2
    rows = own.shape[0]
    unit = rows // zs
    dims = (((0,), (0,)), ((), ()))
    for ref, ring in ((far, 3), (left, 1), (right, 2), (own, 0)):
        block = (ids[0] + SHIFTS[ring] + 4) % 4
        cut = pl.ds(pl.multiple_of(block * rows, rows), rows)
        total = lax.dot_general(t0[:, cut], dj_ref[:half, :], dims, preferred_element_type=jnp.float32)
        total += lax.dot_general(t1[:, cut], dj_ref[half:, :], dims, preferred_element_type=jnp.float32)
        natural[...] = total.astype(jnp.bfloat16)
        for place in range(zs):
            at = pl.multiple_of((ids[1] ^ z_offset(place)) * unit, unit)
            ref[place * unit : (place + 1) * unit, :] = natural[pl.ds(at, unit), :]


def token_grad_kernel(dq_ref, keep_ref, got_ref, w_ref, mine_out, send_out, dj_out):
    dj_out[...] = joined_grads(dq_ref, keep_ref, got_ref)
    half, width = mine_out.shape
    step = width // 4
    dims = (((1,), (1,)), ((), ()))
    for ref, rows in ((send_out, slice(half, None)), (mine_out, slice(0, half))):
        for k in range(4):
            cut = slice(k * step, (k + 1) * step)
            ref[:, cut] = lax.dot_general(
                dj_out[rows, :], w_ref[cut, :], dims, preferred_element_type=jnp.float32
            ).astype(jnp.bfloat16)


def call(kernel, out_shapes, *args, after=(), scratch=(), flops=0, moved=0):
    vmem = pl.BlockSpec(memory_space=pltpu.VMEM)
    smem = pl.BlockSpec(memory_space=pltpu.SMEM)
    in_specs = [smem if a.dtype == jnp.int32 else vmem for a in args]
    in_specs = [pl.BlockSpec(memory_space=pl.ANY)] * len(after) + in_specs
    return pl.pallas_call(
        kernel,
        out_shape=[jax.ShapeDtypeStruct(s, t) for s, t in out_shapes],
        in_specs=in_specs,
        out_specs=[vmem] * len(out_shapes),
        scratch_shapes=[pltpu.VMEM(s, jnp.bfloat16) for s in scratch],
        compiler_params=pltpu.CompilerParams(vmem_limit_bytes=VMEM_LIMIT),
        cost_estimate=pl.CostEstimate(flops=flops, bytes_accessed=moved, transcendentals=0),
    )(*after, *args)


def rows(*parts, after=(), flops=0):
    shape = (len(parts) * parts[0].shape[0], parts[0].shape[1])
    (out,) = call(
        functools.partial(rows_kernel, len(after)), [(shape, parts[0].dtype)], *parts, after=after,
        flops=flops, moved=4 * shape[0] * shape[1],
    )
    return out


def scatter_sum(blocks, *parts, after=()):
    shape = (parts[0].shape[0] // blocks, parts[0].shape[1])
    return call(
        functools.partial(scatter_sum_kernel, len(after), len(parts)),
        [(shape, jnp.float32)] + [(shape, jnp.bfloat16)] * (blocks - 1),
        *parts, after=after, moved=4 * len(parts) * parts[0].shape[0] * shape[1],
    )


def shards(tokens, q_weight, k_weight, v_weight, d_context):
    head = q_weight.shape[1]
    count, width = tokens.shape
    zs = SIZES[1]
    b16, f32 = jnp.bfloat16, jnp.float32
    product = 64 * count * width * head
    ids = jnp.stack([lax.axis_index(a) for a in AXES]).astype(jnp.int32)

    weights = jnp.concatenate([q_weight, k_weight, v_weight], axis=1)
    inv_wide, normed = call(
        norm_kernel, [((count, 128), f32), ((count, width), b16)], tokens,
        flops=4 * count * width, moved=4 * count * width,
    )
    near = rows(weights, *spread(weights, "zl", RADIX), after=(normed,))
    whole = rows(near, *spread(near, "zl", 1))
    w_pieces = (whole, *ring_gather(whole, "x"))
    far = rows(flipped(normed, "zh", 1), after=(whole,), flops=40 * product)
    pair = rows(normed, far, after=w_pieces[1:3])
    t0 = rows(pair, *ring_gather(pair, "y"), after=w_pieces[3:])
    t1 = flipped(t0, "co", 1)

    half = t0.shape[0]
    held = 2 * half
    cosine, sine = (jnp.asarray(t) for t in rope_tables(held, head))
    one_head = ((held, head), b16)
    w_natural, query, kv_mine = call(
        functools.partial(project_kernel, zs),
        [((width, 2 * head), b16), one_head, one_head],
        ids, t0, t1, *w_pieces, cosine, sine,
        flops=product, moved=6 * width * held,
    )
    kv_other = flipped(kv_mine, "co", 1)
    context, d_query, keep, send = call(
        attend_kernel,
        [one_head] * 4,
        ids, query, kv_mine, kv_other, d_context, cosine, sine,
        scratch=[(held, head)] * 2,
        flops=14 * held * held * head, moved=24 * held * head,
    )
    got = flipped(send, "co", 1)
    block = width // SIZES[0]
    p_mine, p_send, joined = call(
        token_grad_kernel,
        [((half, width), b16)] * 2 + [((held, 2 * head), b16)],
        d_query, keep, got, w_natural,
        flops=product, moved=4 * width * held,
    )
    g_blocks = call(
        functools.partial(weight_grad_kernel, zs),
        [((block, 2 * head), b16)] * 4,
        ids, t0, t1, joined,
        scratch=[(block, 2 * head)],
        flops=product, moved=4 * width * held,
    )

    y_blocks = scatter_sum(SIZES[2], p_mine, flipped(p_send, "co", 1), after=(g_blocks[0],))
    kept_t, sent_t = scatter_sum(2, *ring_scatter(y_blocks, "y"))
    from_zh = flipped(sent_t, "zh", 1)
    (grad_tokens,) = call(
        tokens_out_kernel, [((count, width), b16)], tokens, inv_wide, kept_t, from_zh,
        flops=8 * count * width, moved=12 * count * width,
    )

    kept, *sent = scatter_sum(RADIX, *ring_scatter(g_blocks, "x"), after=(y_blocks[0],))
    kept, *sent = scatter_sum(RADIX, kept, *collect(sent, "zl", 1))
    cut = kept.shape[0]
    grads = call(
        weights_out_kernel,
        [((cut, head), f32), ((cut, head // 2), f32), ((cut, head // 2), f32)],
        kept, *collect(sent, "zl", RADIX),
        moved=24 * cut * head,
    )
    return (context, grad_tokens, *grads)


def solution(mesh):
    split = P(DP, TENSOR)
    rows = P(DP + TENSOR, None)
    return jax.shard_map(
        shards,
        mesh=Mesh(mesh.devices.reshape(SIZES), AXES),
        in_specs=(rows, split, split, split, split),
        out_specs=(split, rows, split, split, split),
        check_vma=False,
    )
```

```python
import functools
import math

import jax
import jax.numpy as jnp
import numpy as np
from jax import lax
from jax.experimental import pallas as pl
from jax.experimental.pallas import tpu as pltpu
from jax.sharding import Mesh
from jax.sharding import PartitionSpec as P

SEQ = 16
SHIFTS = (0, -1, 1, 2)
VMEM_LIMIT = 20 * 1024 * 1024

AXES = ("x", "zl", "y", "zh", "co")
SIZES = (4, 16, 4, 2, 2)
DP = ("x", "zl")
TENSOR = ("y", "zh", "co")


def flipped(value, axis, mask):
    size = lax.axis_size(axis)
    return lax.ppermute(value, axis, [(s, s ^ mask) for s in range(size)])


def shifted(value, axis, step):
    size = lax.axis_size(axis)
    return lax.ppermute(value, axis, [(s, (s + step) % size) for s in range(size)])


RADIX = 4


def z_offset(place):
    return place % RADIX * RADIX + place // RADIX


def spread(block, axis, step):
    return tuple(flipped(block, axis, k * step) for k in range(1, RADIX))


def collect(blocks, axis, step):
    return [flipped(block, axis, k * step) for k, block in reversed(list(enumerate(blocks, 1)))]


def ring_gather(block, axis):
    return tuple(shifted(block, axis, -shift) for shift in SHIFTS[1:])


def added(*terms):
    total = terms[0].astype(jnp.float32)
    for term in terms[1:]:
        total = total + term.astype(jnp.float32)
    return total


def rope_tables(rows, head_size):
    position = (np.arange(rows) % SEQ).astype(np.float32)
    exponent = np.arange(head_size // 2).astype(np.float32) * np.float32(2.0 / head_size)
    inverse = np.exp(-exponent * np.log(np.float32(500000.0)))
    angles = position[:, None] * inverse[None, :]
    cosine, sine = np.cos(angles), np.sin(angles)
    return (
        np.concatenate([cosine, cosine], axis=1).astype(np.float32),
        np.concatenate([-sine, sine], axis=1).astype(np.float32),
    )


def half_roll(value):
    return pltpu.roll(value, value.shape[-1] // 2, 1)


def sequence_at(place, ids):
    co, yq, zh = place // 8, place // 2 % 4, place % 2
    y = (ids[2] + SHIFTS[yq] + 4) % 4
    return y * 4 + zh * 2 + (ids[4] ^ co)


def norm_kernel(tokens, inv_out, normed_out):
    inputs = tokens[...].astype(jnp.float32)
    inv = lax.rsqrt(jnp.mean(inputs * inputs, axis=-1, keepdims=True) + 1e-05)
    inv_out[...] = jnp.broadcast_to(inv, inv_out.shape)
    normed_out[...] = (inputs * inv).astype(jnp.bfloat16)


def rows_kernel(first, *refs):
    *parts, out = refs[first:]
    count = parts[0].shape[0]
    for place, ref in enumerate(parts):
        out[place * count : (place + 1) * count, :] = ref[...]


def part_kernel(after, mine, got, *outs):
    count = outs[0].shape[0]
    for place, out in enumerate(outs):
        cut = slice(place * count, (place + 1) * count)
        out[...] = added(mine[cut, :], got[cut, :]).astype(out.dtype)


def pair_kernel(ids, own, left, right, far, keep_out, send_out):
    count = keep_out.shape[0]
    for zh, out in ((ids[3], keep_out), (1 - ids[3], send_out)):
        cut = pl.ds(pl.multiple_of(zh * count, count), count)
        out[...] = added(own[cut, :], left[cut, :], right[cut, :], far[cut, :]).astype(out.dtype)


def scatter_sum_kernel(first, blocks, *refs):
    parts, outs = refs[first:-blocks], refs[-blocks:]
    if len(parts) == 1:
        parts = [parts[0].at[entry] for entry in range(parts[0].shape[0])]
    count = outs[0].shape[0]
    for place, out in enumerate(outs):
        cut = slice(place * count, (place + 1) * count)
        out[...] = added(*(part[cut, :] for part in parts)).astype(out.dtype)


def weights_out_kernel(own, a, b, c, q_out, k_out, v_out):
    total = added(own[...], a[...], b[...], c[...])
    head, half = q_out.shape[1], k_out.shape[1]
    q_out[...] = total[:, :head]
    k_out[...] = total[:, head : head + half]
    v_out[...] = total[:, head + half :]


def tokens_out_kernel(tokens, inv_wide, kept, got, out):
    inputs = tokens[...].astype(jnp.float32)
    d_normed = added(kept[...], got[...])
    inv = inv_wide[:, :1]
    mean = jnp.mean(inputs * d_normed, axis=-1, keepdims=True)
    out[...] = (inv * d_normed - inputs * (inv * inv * inv) * mean).astype(jnp.bfloat16)


def project_kernel(zs, ids, t0, t1, w_own, w_left, w_right, w_far, cos, sin, w_out, q_out, kv_out):
    rows = w_own.shape[0]
    unit = rows // zs
    for ring, ref in enumerate((w_own, w_left, w_right, w_far)):
        block = (ids[0] + SHIFTS[ring] + 4) % 4
        for place in range(zs):
            z = ids[1] ^ z_offset(place)
            at = pl.multiple_of(block * rows + z * unit, unit)
            w_out[pl.ds(at, unit), :] = ref[place * unit : (place + 1) * unit, :]
    totals = []
    for ref in (t0, t1):
        total = None
        for k in range(4):
            cut = slice(k * rows, (k + 1) * rows)
            term = jnp.dot(ref[:, cut], w_out[cut, :], preferred_element_type=jnp.float32)
            total = term if total is None else total + term
        totals.append(total)
    projected = jnp.concatenate(totals, axis=0)
    head = projected.shape[1] // 2
    query = projected[:, :head]
    q_out[...] = (query * cos[...] + half_roll(query) * sin[...]).astype(jnp.bfloat16)
    kv_out[...] = projected[:, head:].astype(jnp.bfloat16)


def attend_kernel(ids, q_ref, mine_ref, other_ref, d_ctx_ref, cos, sin, ctx_out, dq_out, keep_out, send_out, d_ctx, ctx):
    rows, head = q_ref.shape
    half = rows // 2
    scale = 1.0 / math.sqrt(head)
    is_first = ids[4] == 0
    low = lax.broadcasted_iota(jnp.int32, (rows, head), 1) < head // 2
    mine = mine_ref[...].astype(jnp.float32)
    other = jnp.concatenate([other_ref[half:, :], other_ref[:half, :]], axis=0).astype(jnp.float32)
    a = jnp.where(is_first, mine, other)
    b = jnp.where(is_first, other, mine)
    key_raw = jnp.where(low, a, half_roll(b))
    value = jnp.where(low, half_roll(a), b).astype(jnp.bfloat16)
    key = (key_raw * cos[...] + half_roll(key_raw) * sin[...]).astype(jnp.bfloat16)
    query = q_ref[...]
    for place in range(rows // SEQ):
        at = pl.multiple_of(sequence_at(place, ids) * SEQ, SEQ)
        d_ctx[place * SEQ : (place + 1) * SEQ, :] = d_ctx_ref[pl.ds(at, SEQ), :]
    grad_out = d_ctx[...]
    row = lax.broadcasted_iota(jnp.int32, (rows, rows), 0)
    col = lax.broadcasted_iota(jnp.int32, (rows, rows), 1)
    allowed = (row // SEQ == col // SEQ) & (col <= row)
    last = (((1,), (1,)), ((), ()))
    first = (((0,), (0,)), ((), ()))
    dot = functools.partial(lax.dot_general, preferred_element_type=jnp.float32)
    scores = dot(query, key, last) * scale
    masked = jnp.where(allowed, scores, -1e30)
    expd = jnp.exp(masked - jnp.max(masked, axis=-1, keepdims=True))
    probs = expd / jnp.sum(expd, axis=-1, keepdims=True)
    probs_b = probs.astype(jnp.bfloat16)
    ctx[...] = jnp.dot(probs_b, value, preferred_element_type=jnp.float32).astype(jnp.bfloat16)
    for place in range(rows // SEQ):
        at = pl.multiple_of(sequence_at(place, ids) * SEQ, SEQ)
        ctx_out[pl.ds(at, SEQ), :] = ctx[place * SEQ : (place + 1) * SEQ, :]
    d_probs = dot(grad_out, value, last)
    d_scores = probs * (d_probs - jnp.sum(probs * d_probs, axis=-1, keepdims=True)) * scale
    d_scores = d_scores.astype(jnp.bfloat16)
    value_term = dot(probs_b, grad_out, first)
    dq_rot = jnp.dot(d_scores, key, preferred_element_type=jnp.float32)
    dk_rot = dot(d_scores, query, first)
    dq_out[...] = (dq_rot * cos[...] - half_roll(dq_rot) * sin[...]).astype(jnp.bfloat16)
    key_term = dk_rot * cos[...] - half_roll(dk_rot) * sin[...]
    lows = jnp.where(low, key_term, half_roll(value_term))
    highs = jnp.where(low, half_roll(key_term), value_term)
    keep_out[...] = jnp.where(is_first, lows, highs).astype(jnp.bfloat16)
    send_out[...] = jnp.where(is_first, highs, lows).astype(jnp.bfloat16)


def joined_grads(dq_ref, keep_ref, got_ref):
    half = dq_ref.shape[0] // 2
    got = jnp.concatenate([got_ref[half:, :], got_ref[:half, :]], axis=0)
    d_kv = (keep_ref[...].astype(jnp.float32) + got.astype(jnp.float32)).astype(jnp.bfloat16)
    return jnp.concatenate([dq_ref[...], d_kv], axis=1)


def weight_grad_kernel(zs, ids, t0, t1, dj_ref, out, natural):
    half = dj_ref.shape[0] // 2
    blocks, rows = out.shape[:2]
    unit = rows // zs
    dims = (((0,), (0,)), ((), ()))
    for block in range(blocks):
        cut = slice(block * rows, (block + 1) * rows)
        total = lax.dot_general(t0[:, cut], dj_ref[:half, :], dims, preferred_element_type=jnp.float32)
        total += lax.dot_general(t1[:, cut], dj_ref[half:, :], dims, preferred_element_type=jnp.float32)
        natural[...] = total.astype(jnp.bfloat16)
        for place in range(zs):
            at = pl.multiple_of((ids[1] ^ z_offset(place)) * unit, unit)
            out[block, place * unit : (place + 1) * unit, :] = natural[pl.ds(at, unit), :]


def token_grad_kernel(dq_ref, keep_ref, got_ref, w_ref, mine_out, send_out, dj_out):
    dj_out[...] = joined_grads(dq_ref, keep_ref, got_ref)
    half, width = mine_out.shape
    step = width // 4
    dims = (((1,), (1,)), ((), ()))
    for ref, rows in ((send_out, slice(half, None)), (mine_out, slice(0, half))):
        for k in range(4):
            cut = slice(k * step, (k + 1) * step)
            ref[:, cut] = lax.dot_general(
                dj_out[rows, :], w_ref[cut, :], dims, preferred_element_type=jnp.float32
            ).astype(jnp.bfloat16)


def call(kernel, out_shapes, *args, after=(), scratch=(), flops=0, moved=0):
    vmem = pl.BlockSpec(memory_space=pltpu.VMEM)
    smem = pl.BlockSpec(memory_space=pltpu.SMEM)
    in_specs = [smem if a.dtype == jnp.int32 else vmem for a in args]
    in_specs = [pl.BlockSpec(memory_space=pl.ANY)] * len(after) + in_specs
    return pl.pallas_call(
        kernel,
        out_shape=[jax.ShapeDtypeStruct(s, t) for s, t in out_shapes],
        in_specs=in_specs,
        out_specs=[vmem] * len(out_shapes),
        scratch_shapes=[pltpu.VMEM(s, jnp.bfloat16) for s in scratch],
        compiler_params=pltpu.CompilerParams(vmem_limit_bytes=VMEM_LIMIT),
        cost_estimate=pl.CostEstimate(flops=flops, bytes_accessed=moved, transcendentals=0),
    )(*after, *args)


def rows(*parts, after=(), flops=0):
    shape = (len(parts) * parts[0].shape[0], parts[0].shape[1])
    (out,) = call(
        functools.partial(rows_kernel, len(after)), [(shape, parts[0].dtype)], *parts, after=after,
        flops=flops, moved=4 * shape[0] * shape[1],
    )
    return out


def scatter_sum(blocks, *parts, after=()):
    shape = (parts[0].shape[-2] // blocks, parts[0].shape[-1])
    return call(
        functools.partial(scatter_sum_kernel, len(after), blocks),
        [(shape, jnp.float32)] + [(shape, jnp.bfloat16)] * (blocks - 1),
        *parts, after=after, moved=16 * blocks * shape[0] * shape[1],
    )


def shards(tokens, q_weight, k_weight, v_weight, d_context):
    head = q_weight.shape[1]
    count, width = tokens.shape
    zs = SIZES[1]
    b16, f32 = jnp.bfloat16, jnp.float32
    product = 64 * count * width * head
    ids = jnp.stack([lax.axis_index(a) for a in AXES]).astype(jnp.int32)

    weights = jnp.concatenate([q_weight, k_weight, v_weight], axis=1)
    inv_wide, normed = call(
        norm_kernel, [((count, 128), f32), ((count, width), b16)], tokens,
        flops=4 * count * width, moved=4 * count * width,
    )
    near = rows(weights, *spread(weights, "zl", RADIX), after=(normed,))
    whole = rows(near, *spread(near, "zl", 1))
    w_pieces = (whole, *ring_gather(whole, "x"))
    both = lax.all_to_all(jnp.stack([normed, normed]), "zh", 0, 0).reshape(2 * count, width)
    pair = rows(both, after=(whole,), flops=40 * product)
    t0 = rows(pair, *ring_gather(pair, "y"), after=w_pieces[1:])
    t1 = flipped(t0, "co", 1)

    half = t0.shape[0]
    held = 2 * half
    cosine, sine = (jnp.asarray(t) for t in rope_tables(held, head))
    one_head = ((held, head), b16)
    w_natural, query, kv_mine = call(
        functools.partial(project_kernel, zs),
        [((width, 2 * head), b16), one_head, one_head],
        ids, t0, t1, *w_pieces, cosine, sine,
        flops=product, moved=6 * width * held,
    )
    kv_other = flipped(kv_mine, "co", 1)
    context, d_query, keep, send = call(
        attend_kernel,
        [one_head] * 4,
        ids, query, kv_mine, kv_other, d_context, cosine, sine,
        scratch=[(held, head)] * 2,
        flops=14 * held * held * head, moved=24 * held * head,
    )
    got = flipped(send, "co", 1)
    block = width // SIZES[0]
    p_mine, p_send, joined = call(
        token_grad_kernel,
        [((half, width), b16)] * 2 + [((held, 2 * head), b16)],
        d_query, keep, got, w_natural,
        flops=product, moved=4 * width * held,
    )
    (g_blocks,) = call(
        functools.partial(weight_grad_kernel, zs),
        [((SIZES[0], block, 2 * head), b16)],
        ids, t0, t1, joined,
        scratch=[(block, 2 * head)],
        flops=product, moved=4 * width * held,
    )

    y_own, *y_sent = call(
        part_kernel, [((2 * count, width), f32)] + [((2 * count, width), b16)] * 3, p_mine, flipped(p_send, "co", 1),
        after=(g_blocks,), moved=24 * half * width,
    )
    y_got = [shifted(sent, "y", shift) for sent, shift in zip(y_sent, SHIFTS[1:])]
    kept_t, sent_t = call(
        pair_kernel, [((count, width), f32), ((count, width), b16)], ids, y_own, *y_got, moved=24 * count * width,
    )
    from_zh = flipped(sent_t, "zh", 1)
    (grad_tokens,) = call(
        tokens_out_kernel, [((count, width), b16)], tokens, inv_wide, kept_t, from_zh,
        flops=40 * product, moved=12 * count * width,
    )

    kept, *sent = scatter_sum(RADIX, lax.all_to_all(g_blocks, "x", 0, 0), after=(sent_t,))
    kept, *sent = scatter_sum(RADIX, kept, *collect(sent, "zl", 1))
    cut = kept.shape[0]
    grads = call(
        weights_out_kernel,
        [((cut, head), f32), ((cut, head // 2), f32), ((cut, head // 2), f32)],
        kept, *collect(sent, "zl", RADIX),
        moved=24 * cut * head,
    )
    return (context, grad_tokens, *grads)


def solution(mesh):
    split = P(DP, TENSOR)
    rows = P(DP + TENSOR, None)
    return jax.shard_map(
        shards,
        mesh=Mesh(mesh.devices.reshape(SIZES), AXES),
        in_specs=(rows, split, split, split, split),
        out_specs=(split, rows, split, split, split),
        check_vma=False,
    )
```

```python
import functools
import math

import jax
import jax.numpy as jnp
import numpy as np
from jax import lax
from jax.experimental import pallas as pl
from jax.experimental.pallas import tpu as pltpu
from jax.sharding import Mesh
from jax.sharding import PartitionSpec as P

SEQ = 16
SHIFTS = (0, -1, 1, 2)
VMEM_LIMIT = 20 * 1024 * 1024

AXES = ("x", "zl", "y", "zh", "co")
SIZES = (4, 16, 4, 2, 2)
DP = ("x", "zl")
TENSOR = ("y", "zh", "co")


def flipped(value, axis, mask):
    size = lax.axis_size(axis)
    return lax.ppermute(value, axis, [(s, s ^ mask) for s in range(size)])


def shifted(value, axis, step):
    size = lax.axis_size(axis)
    return lax.ppermute(value, axis, [(s, (s + step) % size) for s in range(size)])


RADIX = 4


def z_offset(place):
    far = place % RADIX
    return (far & 1) * 2 * RADIX + (far >> 1) * RADIX + place // RADIX


def spread(block, axis, step):
    return tuple(flipped(block, axis, k * step) for k in range(1, RADIX))


def collect(blocks, axis, step):
    return [flipped(block, axis, k * step) for k, block in reversed(list(enumerate(blocks, 1)))]


def ring_gather(block, axis):
    return tuple(shifted(block, axis, -shift) for shift in SHIFTS[1:])


def added(*terms):
    total = terms[0].astype(jnp.float32)
    for term in terms[1:]:
        total = total + term.astype(jnp.float32)
    return total


def rope_tables(rows, head_size):
    position = (np.arange(rows) % SEQ).astype(np.float32)
    exponent = np.arange(head_size // 2).astype(np.float32) * np.float32(2.0 / head_size)
    inverse = np.exp(-exponent * np.log(np.float32(500000.0)))
    angles = position[:, None] * inverse[None, :]
    cosine, sine = np.cos(angles), np.sin(angles)
    return (
        np.concatenate([cosine, cosine], axis=1).astype(np.float32),
        np.concatenate([-sine, sine], axis=1).astype(np.float32),
    )


def half_roll(value):
    return pltpu.roll(value, value.shape[-1] // 2, 1)


def sequence_at(place, ids):
    co, yq, zh = place // 8, place // 2 % 4, place % 2
    y = (ids[2] + SHIFTS[yq] + 4) % 4
    return y * 4 + (ids[3] ^ zh) * 2 + (ids[4] ^ co)


def norm_kernel(tokens, inv_out, normed_out):
    inputs = tokens[...].astype(jnp.float32)
    inv = lax.rsqrt(jnp.mean(inputs * inputs, axis=-1, keepdims=True) + 1e-05)
    inv_out[...] = jnp.broadcast_to(inv, inv_out.shape)
    normed_out[...] = (inputs * inv).astype(jnp.bfloat16)


def rows_kernel(first, *refs):
    *parts, out = refs[first:]
    count = parts[0].shape[0]
    for place, ref in enumerate(parts):
        out[place * count : (place + 1) * count, :] = ref[...]


def part_kernel(after, mine, got, *outs):
    count = outs[0].shape[0]
    for place, out in enumerate(outs):
        cut = slice(place * count, (place + 1) * count)
        out[...] = added(mine[cut, :], got[cut, :]).astype(out.dtype)


def pair_kernel(own, left, right, far, keep_out, send_out):
    count = keep_out.shape[0]
    for place, out in enumerate((keep_out, send_out)):
        cut = slice(place * count, (place + 1) * count)
        out[...] = added(own[cut, :], left[cut, :], right[cut, :], far[cut, :]).astype(out.dtype)


def scatter_sum_kernel(first, blocks, *refs):
    parts, outs = refs[first:-blocks], refs[-blocks:]
    if len(parts) == 1:
        parts = [parts[0].at[entry] for entry in range(parts[0].shape[0])]
    count = outs[0].shape[0]
    for place, out in enumerate(outs):
        cut = slice(place * count, (place + 1) * count)
        out[...] = added(*(part[cut, :] for part in parts)).astype(out.dtype)


def weights_out_kernel(own, got, q_out, k_out, v_out):
    total = added(own[...], got[...])
    head, half = q_out.shape[1], k_out.shape[1]
    q_out[...] = total[:, :head]
    k_out[...] = total[:, head : head + half]
    v_out[...] = total[:, head + half :]


def tokens_out_kernel(tokens, inv_wide, kept, got, out):
    inputs = tokens[...].astype(jnp.float32)
    d_normed = added(kept[...], got[...])
    inv = inv_wide[:, :1]
    mean = jnp.mean(inputs * d_normed, axis=-1, keepdims=True)
    out[...] = (inv * d_normed - inputs * (inv * inv * inv) * mean).astype(jnp.bfloat16)


def project_kernel(zs, ids, t0, t1, w_own, w_left, w_right, w_far, cos, sin, w_out, q_out, kv_out):
    rows = w_own.shape[0]
    unit = rows // zs
    for ring, ref in enumerate((w_own, w_left, w_right, w_far)):
        block = (ids[0] + SHIFTS[ring] + 4) % 4
        for place in range(zs):
            z = ids[1] ^ z_offset(place)
            at = pl.multiple_of(block * rows + z * unit, unit)
            w_out[pl.ds(at, unit), :] = ref[place * unit : (place + 1) * unit, :]
    totals = []
    for ref in (t0, t1):
        total = None
        for k in range(4):
            cut = slice(k * rows, (k + 1) * rows)
            term = jnp.dot(ref[:, cut], w_out[cut, :], preferred_element_type=jnp.float32)
            total = term if total is None else total + term
        totals.append(total)
    projected = jnp.concatenate(totals, axis=0)
    head = projected.shape[1] // 2
    query = projected[:, :head]
    q_out[...] = (query * cos[...] + half_roll(query) * sin[...]).astype(jnp.bfloat16)
    kv_out[...] = projected[:, head:].astype(jnp.bfloat16)


def attend_kernel(ids, q_ref, mine_ref, other_ref, d_ctx_ref, cos, sin, ctx_out, dq_out, keep_out, send_out, d_ctx, ctx):
    rows, head = q_ref.shape
    half = rows // 2
    scale = 1.0 / math.sqrt(head)
    is_first = ids[4] == 0
    low = lax.broadcasted_iota(jnp.int32, (rows, head), 1) < head // 2
    mine = mine_ref[...].astype(jnp.float32)
    other = jnp.concatenate([other_ref[half:, :], other_ref[:half, :]], axis=0).astype(jnp.float32)
    a = jnp.where(is_first, mine, other)
    b = jnp.where(is_first, other, mine)
    key_raw = jnp.where(low, a, half_roll(b))
    value = jnp.where(low, half_roll(a), b).astype(jnp.bfloat16)
    key = (key_raw * cos[...] + half_roll(key_raw) * sin[...]).astype(jnp.bfloat16)
    query = q_ref[...]
    for place in range(rows // SEQ):
        at = pl.multiple_of(sequence_at(place, ids) * SEQ, SEQ)
        d_ctx[place * SEQ : (place + 1) * SEQ, :] = d_ctx_ref[pl.ds(at, SEQ), :]
    grad_out = d_ctx[...]
    row = lax.broadcasted_iota(jnp.int32, (rows, rows), 0)
    col = lax.broadcasted_iota(jnp.int32, (rows, rows), 1)
    allowed = (row // SEQ == col // SEQ) & (col <= row)
    last = (((1,), (1,)), ((), ()))
    first = (((0,), (0,)), ((), ()))
    dot = functools.partial(lax.dot_general, preferred_element_type=jnp.float32)
    scores = dot(query, key, last) * scale
    masked = jnp.where(allowed, scores, -1e30)
    expd = jnp.exp(masked - jnp.max(masked, axis=-1, keepdims=True))
    probs = expd / jnp.sum(expd, axis=-1, keepdims=True)
    probs_b = probs.astype(jnp.bfloat16)
    ctx[...] = jnp.dot(probs_b, value, preferred_element_type=jnp.float32).astype(jnp.bfloat16)
    for place in range(rows // SEQ):
        at = pl.multiple_of(sequence_at(place, ids) * SEQ, SEQ)
        ctx_out[pl.ds(at, SEQ), :] = ctx[place * SEQ : (place + 1) * SEQ, :]
    d_probs = dot(grad_out, value, last)
    d_scores = probs * (d_probs - jnp.sum(probs * d_probs, axis=-1, keepdims=True)) * scale
    d_scores = d_scores.astype(jnp.bfloat16)
    value_term = dot(probs_b, grad_out, first)
    dq_rot = jnp.dot(d_scores, key, preferred_element_type=jnp.float32)
    dk_rot = dot(d_scores, query, first)
    dq_out[...] = (dq_rot * cos[...] - half_roll(dq_rot) * sin[...]).astype(jnp.bfloat16)
    key_term = dk_rot * cos[...] - half_roll(dk_rot) * sin[...]
    lows = jnp.where(low, key_term, half_roll(value_term))
    highs = jnp.where(low, half_roll(key_term), value_term)
    keep_out[...] = jnp.where(is_first, lows, highs).astype(jnp.bfloat16)
    send_out[...] = jnp.where(is_first, highs, lows).astype(jnp.bfloat16)


def joined_grads(dq_ref, keep_ref, got_ref):
    half = dq_ref.shape[0] // 2
    got = jnp.concatenate([got_ref[half:, :], got_ref[:half, :]], axis=0)
    d_kv = (keep_ref[...].astype(jnp.float32) + got.astype(jnp.float32)).astype(jnp.bfloat16)
    return jnp.concatenate([dq_ref[...], d_kv], axis=1)


def weight_grad_kernel(zs, ids, t0, t1, dj_ref, out, natural):
    half = dj_ref.shape[0] // 2
    blocks, rows = out.shape[:2]
    unit = rows // zs
    dims = (((0,), (0,)), ((), ()))
    for block in range(blocks):
        cut = slice(block * rows, (block + 1) * rows)
        total = lax.dot_general(t0[:, cut], dj_ref[:half, :], dims, preferred_element_type=jnp.float32)
        total += lax.dot_general(t1[:, cut], dj_ref[half:, :], dims, preferred_element_type=jnp.float32)
        natural[...] = total.astype(jnp.bfloat16)
        for place in range(zs):
            at = pl.multiple_of((ids[1] ^ z_offset(place)) * unit, unit)
            out[block, place * unit : (place + 1) * unit, :] = natural[pl.ds(at, unit), :]


def token_grad_kernel(dq_ref, keep_ref, got_ref, w_ref, mine_out, send_out, dj_out):
    dj_out[...] = joined_grads(dq_ref, keep_ref, got_ref)
    half, width = mine_out.shape
    step = width // 4
    dims = (((1,), (1,)), ((), ()))
    for ref, rows in ((send_out, slice(half, None)), (mine_out, slice(0, half))):
        for k in range(4):
            cut = slice(k * step, (k + 1) * step)
            ref[:, cut] = lax.dot_general(
                dj_out[rows, :], w_ref[cut, :], dims, preferred_element_type=jnp.float32
            ).astype(jnp.bfloat16)


def call(kernel, out_shapes, *args, after=(), scratch=(), flops=0, moved=0):
    vmem = pl.BlockSpec(memory_space=pltpu.VMEM)
    smem = pl.BlockSpec(memory_space=pltpu.SMEM)
    in_specs = [smem if a.dtype == jnp.int32 else vmem for a in args]
    in_specs = [pl.BlockSpec(memory_space=pl.ANY)] * len(after) + in_specs
    return pl.pallas_call(
        kernel,
        out_shape=[jax.ShapeDtypeStruct(s, t) for s, t in out_shapes],
        in_specs=in_specs,
        out_specs=[vmem] * len(out_shapes),
        scratch_shapes=[pltpu.VMEM(s, jnp.bfloat16) for s in scratch],
        compiler_params=pltpu.CompilerParams(vmem_limit_bytes=VMEM_LIMIT),
        cost_estimate=pl.CostEstimate(flops=flops, bytes_accessed=moved, transcendentals=0),
    )(*after, *args)


def rows(*parts, after=(), flops=0):
    shape = (len(parts) * parts[0].shape[0], parts[0].shape[1])
    (out,) = call(
        functools.partial(rows_kernel, len(after)), [(shape, parts[0].dtype)], *parts, after=after,
        flops=flops, moved=4 * shape[0] * shape[1],
    )
    return out


def scatter_sum(blocks, *parts, after=()):
    shape = (parts[0].shape[-2] // blocks, parts[0].shape[-1])
    return call(
        functools.partial(scatter_sum_kernel, len(after), blocks),
        [(shape, jnp.float32)] + [(shape, jnp.bfloat16)] * (blocks - 1),
        *parts, after=after, moved=16 * blocks * shape[0] * shape[1],
    )


def shards(tokens, q_weight, k_weight, v_weight, d_context):
    head = q_weight.shape[1]
    count, width = tokens.shape
    zs = SIZES[1]
    b16, f32 = jnp.bfloat16, jnp.float32
    product = 64 * count * width * head
    ids = jnp.stack([lax.axis_index(a) for a in AXES]).astype(jnp.int32)

    weights = jnp.concatenate([q_weight, k_weight, v_weight], axis=1)
    inv_wide, normed = call(
        norm_kernel, [((count, 128), f32), ((count, width), b16)], tokens,
        flops=4 * count * width, moved=4 * count * width,
    )
    near = rows(weights, flipped(weights, "zl", 2 * RADIX), after=(normed,))
    near = rows(near, flipped(near, "zl", RADIX))
    whole = rows(near, *spread(near, "zl", 1))
    w_pieces = (whole, *ring_gather(whole, "x"))
    far = rows(flipped(normed, "zh", 1), after=(whole,), flops=40 * product)
    pair = rows(normed, far, after=w_pieces[1:3])
    t0 = rows(pair, *ring_gather(pair, "y"), after=w_pieces[3:])
    t1 = flipped(t0, "co", 1)

    half = t0.shape[0]
    held = 2 * half
    cosine, sine = (jnp.asarray(t) for t in rope_tables(held, head))
    one_head = ((held, head), b16)
    w_natural, query, kv_mine = call(
        functools.partial(project_kernel, zs),
        [((width, 2 * head), b16), one_head, one_head],
        ids, t0, t1, *w_pieces, cosine, sine,
        flops=product, moved=6 * width * held,
    )
    kv_other = flipped(kv_mine, "co", 1)
    context, d_query, keep, send = call(
        attend_kernel,
        [one_head] * 4,
        ids, query, kv_mine, kv_other, d_context, cosine, sine,
        scratch=[(held, head)] * 2,
        flops=14 * held * held * head, moved=24 * held * head,
    )
    got = flipped(send, "co", 1)
    block = width // SIZES[0]
    p_mine, p_send, joined = call(
        token_grad_kernel,
        [((half, width), b16)] * 2 + [((held, 2 * head), b16)],
        d_query, keep, got, w_natural,
        flops=product, moved=4 * width * held,
    )
    (g_blocks,) = call(
        functools.partial(weight_grad_kernel, zs),
        [((SIZES[0], block, 2 * head), b16)],
        ids, t0, t1, joined,
        scratch=[(block, 2 * head)],
        flops=product, moved=4 * width * held,
    )

    y_own, *y_sent = call(
        part_kernel, [((2 * count, width), f32)] + [((2 * count, width), b16)] * 3, p_mine, flipped(p_send, "co", 1),
        after=(g_blocks,), moved=24 * half * width,
    )
    y_got = [shifted(sent, "y", shift) for sent, shift in zip(y_sent, SHIFTS[1:])]
    kept_t, sent_t = call(
        pair_kernel, [((count, width), f32), ((count, width), b16)], y_own, *y_got, moved=24 * count * width,
    )
    from_zh = flipped(sent_t, "zh", 1)
    (grad_tokens,) = call(
        tokens_out_kernel, [((count, width), b16)], tokens, inv_wide, kept_t, from_zh,
        flops=40 * product, moved=12 * count * width,
    )

    kept, *sent = scatter_sum(RADIX, lax.all_to_all(g_blocks, "x", 0, 0), after=(sent_t,))
    kept, sent = scatter_sum(2, kept, *collect(sent, "zl", 1))
    kept, sent = scatter_sum(2, kept, flipped(sent, "zl", RADIX))
    cut = kept.shape[0]
    grads = call(
        weights_out_kernel,
        [((cut, head), f32), ((cut, head // 2), f32), ((cut, head // 2), f32)],
        kept, flipped(sent, "zl", 2 * RADIX),
        moved=12 * cut * head,
    )
    return (context, grad_tokens, *grads)


def solution(mesh):
    split = P(DP, TENSOR)
    rows = P(DP + TENSOR, None)
    return jax.shard_map(
        shards,
        mesh=Mesh(mesh.devices.reshape(SIZES), AXES),
        in_specs=(rows, split, split, split, split),
        out_specs=(split, rows, split, split, split),
        check_vma=False,
    )
```

```python
import functools
import math

import jax
import jax.numpy as jnp
import numpy as np
from jax import lax
from jax.experimental import pallas as pl
from jax.experimental.pallas import tpu as pltpu
from jax.sharding import Mesh
from jax.sharding import PartitionSpec as P

SEQ = 16
SHIFTS = (0, -1, 1, 2)
VMEM_LIMIT = 20 * 1024 * 1024

AXES = ("x", "zl", "y", "zh", "co")
SIZES = (4, 16, 4, 2, 2)
DP = ("x", "zl")
TENSOR = ("y", "zh", "co")


def flipped(value, axis, mask):
    size = lax.axis_size(axis)
    return lax.ppermute(value, axis, [(s, s ^ mask) for s in range(size)])


def shifted(value, axis, step):
    size = lax.axis_size(axis)
    return lax.ppermute(value, axis, [(s, (s + step) % size) for s in range(size)])


RADIX = 4


def z_offset(place):
    return place % RADIX * RADIX + place // RADIX


def spread(block, axis, step):
    return tuple(flipped(block, axis, k * step) for k in range(1, RADIX))


def collect(blocks, axis, step):
    return [flipped(block, axis, k * step) for k, block in reversed(list(enumerate(blocks, 1)))]


def ring_gather(block, axis):
    return tuple(shifted(block, axis, -shift) for shift in SHIFTS[1:])


def added(*terms):
    total = terms[0].astype(jnp.float32)
    for term in terms[1:]:
        total = total + term.astype(jnp.float32)
    return total


def rope_tables(rows, head_size):
    position = (np.arange(rows) % SEQ).astype(np.float32)
    exponent = np.arange(head_size // 2).astype(np.float32) * np.float32(2.0 / head_size)
    inverse = np.exp(-exponent * np.log(np.float32(500000.0)))
    angles = position[:, None] * inverse[None, :]
    cosine, sine = np.cos(angles), np.sin(angles)
    return (
        np.concatenate([cosine, cosine], axis=1).astype(np.float32),
        np.concatenate([-sine, sine], axis=1).astype(np.float32),
    )


def half_roll(value):
    return pltpu.roll(value, value.shape[-1] // 2, 1)


def sequence_at(place, ids):
    co, yq, zh = place // 8, place // 2 % 4, place % 2
    y = (ids[2] + SHIFTS[yq] + 4) % 4
    return y * 4 + (ids[3] ^ zh) * 2 + (ids[4] ^ co)


def norm_kernel(tokens, inv_out, normed_out):
    inputs = tokens[...].astype(jnp.float32)
    inv = lax.rsqrt(jnp.mean(inputs * inputs, axis=-1, keepdims=True) + 1e-05)
    inv_out[...] = jnp.broadcast_to(inv, inv_out.shape)
    normed_out[...] = (inputs * inv).astype(jnp.bfloat16)


def rows_kernel(first, order, *refs):
    *parts, out = refs[first:]
    count = parts[0].shape[0]
    for place, ref in enumerate(parts[::order]):
        out[place * count : (place + 1) * count, :] = ref[...]


def part_kernel(after, mine, got, *outs):
    count = outs[0].shape[0]
    for place, out in enumerate(outs):
        cut = slice(place * count, (place + 1) * count)
        out[...] = added(mine[cut, :], got[cut, :]).astype(out.dtype)


def pair_kernel(own, left, right, far, keep_out, send_out):
    count = keep_out.shape[0]
    for place, out in enumerate((keep_out, send_out)):
        cut = slice(place * count, (place + 1) * count)
        out[...] = added(own[cut, :], left[cut, :], right[cut, :], far[cut, :]).astype(out.dtype)


def scatter_sum_kernel(first, blocks, *refs):
    parts, outs = refs[first:-blocks], refs[-blocks:]
    if len(parts) == 1:
        parts = [parts[0].at[entry] for entry in range(parts[0].shape[0])]
    count = outs[0].shape[0]
    for place, out in enumerate(outs):
        cut = slice(place * count, (place + 1) * count)
        out[...] = added(*(part[cut, :] for part in parts)).astype(out.dtype)


def weights_out_kernel(own, a, b, c, q_out, k_out, v_out):
    total = added(own[...], a[...], b[...], c[...])
    head, half = q_out.shape[1], k_out.shape[1]
    q_out[...] = total[:, :head]
    k_out[...] = total[:, head : head + half]
    v_out[...] = total[:, head + half :]


def tokens_out_kernel(tokens, inv_wide, kept, got, out):
    inputs = tokens[...].astype(jnp.float32)
    d_normed = added(kept[...], got[...])
    inv = inv_wide[:, :1]
    mean = jnp.mean(inputs * d_normed, axis=-1, keepdims=True)
    out[...] = (inv * d_normed - inputs * (inv * inv * inv) * mean).astype(jnp.bfloat16)


def project_kernel(zs, ids, t0, t1, w_own, w_left, w_right, w_far, cos, sin, w_out, q_out, kv_out):
    rows = w_own.shape[0]
    unit = rows // zs
    for ring, ref in enumerate((w_own, w_left, w_right, w_far)):
        block = (ids[0] + SHIFTS[ring] + 4) % 4
        for place in range(zs):
            z = ids[1] ^ z_offset(place)
            at = pl.multiple_of(block * rows + z * unit, unit)
            w_out[pl.ds(at, unit), :] = ref[place * unit : (place + 1) * unit, :]
    totals = []
    for ref in (t0, t1):
        total = None
        for k in range(4):
            cut = slice(k * rows, (k + 1) * rows)
            term = jnp.dot(ref[:, cut], w_out[cut, :], preferred_element_type=jnp.float32)
            total = term if total is None else total + term
        totals.append(total)
    projected = jnp.concatenate(totals, axis=0)
    head = projected.shape[1] // 2
    query = projected[:, :head]
    q_out[...] = (query * cos[...] + half_roll(query) * sin[...]).astype(jnp.bfloat16)
    kv_out[...] = projected[:, head:].astype(jnp.bfloat16)


def attend_kernel(ids, q_ref, mine_ref, other_ref, d_ctx_ref, cos, sin, ctx_out, dq_out, keep_out, send_out, d_ctx, ctx):
    rows, head = q_ref.shape
    half = rows // 2
    scale = 1.0 / math.sqrt(head)
    is_first = ids[4] == 0
    low = lax.broadcasted_iota(jnp.int32, (rows, head), 1) < head // 2
    mine = mine_ref[...].astype(jnp.float32)
    other = jnp.concatenate([other_ref[half:, :], other_ref[:half, :]], axis=0).astype(jnp.float32)
    a = jnp.where(is_first, mine, other)
    b = jnp.where(is_first, other, mine)
    key_raw = jnp.where(low, a, half_roll(b))
    value = jnp.where(low, half_roll(a), b).astype(jnp.bfloat16)
    key = (key_raw * cos[...] + half_roll(key_raw) * sin[...]).astype(jnp.bfloat16)
    query = q_ref[...]
    for place in range(rows // SEQ):
        at = pl.multiple_of(sequence_at(place, ids) * SEQ, SEQ)
        d_ctx[place * SEQ : (place + 1) * SEQ, :] = d_ctx_ref[pl.ds(at, SEQ), :]
    grad_out = d_ctx[...]
    row = lax.broadcasted_iota(jnp.int32, (rows, rows), 0)
    col = lax.broadcasted_iota(jnp.int32, (rows, rows), 1)
    allowed = (row // SEQ == col // SEQ) & (col <= row)
    last = (((1,), (1,)), ((), ()))
    first = (((0,), (0,)), ((), ()))
    dot = functools.partial(lax.dot_general, preferred_element_type=jnp.float32)
    scores = dot(query, key, last) * scale
    masked = jnp.where(allowed, scores, -1e30)
    expd = jnp.exp(masked - jnp.max(masked, axis=-1, keepdims=True))
    probs = expd / jnp.sum(expd, axis=-1, keepdims=True)
    probs_b = probs.astype(jnp.bfloat16)
    ctx[...] = jnp.dot(probs_b, value, preferred_element_type=jnp.float32).astype(jnp.bfloat16)
    for place in range(rows // SEQ):
        at = pl.multiple_of(sequence_at(place, ids) * SEQ, SEQ)
        ctx_out[pl.ds(at, SEQ), :] = ctx[place * SEQ : (place + 1) * SEQ, :]
    d_probs = dot(grad_out, value, last)
    d_scores = probs * (d_probs - jnp.sum(probs * d_probs, axis=-1, keepdims=True)) * scale
    d_scores = d_scores.astype(jnp.bfloat16)
    value_term = dot(probs_b, grad_out, first)
    dq_rot = jnp.dot(d_scores, key, preferred_element_type=jnp.float32)
    dk_rot = dot(d_scores, query, first)
    dq_out[...] = (dq_rot * cos[...] - half_roll(dq_rot) * sin[...]).astype(jnp.bfloat16)
    key_term = dk_rot * cos[...] - half_roll(dk_rot) * sin[...]
    lows = jnp.where(low, key_term, half_roll(value_term))
    highs = jnp.where(low, half_roll(key_term), value_term)
    keep_out[...] = jnp.where(is_first, lows, highs).astype(jnp.bfloat16)
    send_out[...] = jnp.where(is_first, highs, lows).astype(jnp.bfloat16)


def joined_grads(dq_ref, keep_ref, got_ref):
    half = dq_ref.shape[0] // 2
    got = jnp.concatenate([got_ref[half:, :], got_ref[:half, :]], axis=0)
    d_kv = (keep_ref[...].astype(jnp.float32) + got.astype(jnp.float32)).astype(jnp.bfloat16)
    return jnp.concatenate([dq_ref[...], d_kv], axis=1)


def weight_grad_kernel(zs, ids, t0, t1, dj_ref, out, natural):
    half = dj_ref.shape[0] // 2
    blocks, rows = out.shape[:2]
    unit = rows // zs
    dims = (((0,), (0,)), ((), ()))
    for block in range(blocks):
        cut = slice(block * rows, (block + 1) * rows)
        total = lax.dot_general(t0[:, cut], dj_ref[:half, :], dims, preferred_element_type=jnp.float32)
        total += lax.dot_general(t1[:, cut], dj_ref[half:, :], dims, preferred_element_type=jnp.float32)
        natural[...] = total.astype(jnp.bfloat16)
        for place in range(zs):
            at = pl.multiple_of((ids[1] ^ z_offset(place)) * unit, unit)
            out[block, place * unit : (place + 1) * unit, :] = natural[pl.ds(at, unit), :]


def token_grad_kernel(dq_ref, keep_ref, got_ref, w_ref, mine_out, send_out, dj_out):
    dj_out[...] = joined_grads(dq_ref, keep_ref, got_ref)
    half, width = mine_out.shape
    step = width // 4
    dims = (((1,), (1,)), ((), ()))
    for ref, rows in ((send_out, slice(half, None)), (mine_out, slice(0, half))):
        for k in range(4):
            cut = slice(k * step, (k + 1) * step)
            ref[:, cut] = lax.dot_general(
                dj_out[rows, :], w_ref[cut, :], dims, preferred_element_type=jnp.float32
            ).astype(jnp.bfloat16)


def call(kernel, out_shapes, *args, after=(), scratch=(), flops=0, moved=0):
    vmem = pl.BlockSpec(memory_space=pltpu.VMEM)
    smem = pl.BlockSpec(memory_space=pltpu.SMEM)
    in_specs = [smem if a.dtype == jnp.int32 else vmem for a in args]
    in_specs = [pl.BlockSpec(memory_space=pl.ANY)] * len(after) + in_specs
    return pl.pallas_call(
        kernel,
        out_shape=[jax.ShapeDtypeStruct(s, t) for s, t in out_shapes],
        in_specs=in_specs,
        out_specs=[vmem] * len(out_shapes),
        scratch_shapes=[pltpu.VMEM(s, jnp.bfloat16) for s in scratch],
        compiler_params=pltpu.CompilerParams(vmem_limit_bytes=VMEM_LIMIT),
        cost_estimate=pl.CostEstimate(flops=flops, bytes_accessed=moved, transcendentals=0),
    )(*after, *args)


def rows(*parts, after=(), last_first=False, flops=0):
    shape = (len(parts) * parts[0].shape[0], parts[0].shape[1])
    (out,) = call(
        functools.partial(rows_kernel, len(after), -1 if last_first else 1), [(shape, parts[0].dtype)], *parts, after=after,
        flops=flops, moved=4 * shape[0] * shape[1],
    )
    return out


def scatter_sum(blocks, *parts, after=()):
    shape = (parts[0].shape[-2] // blocks, parts[0].shape[-1])
    return call(
        functools.partial(scatter_sum_kernel, len(after), blocks),
        [(shape, jnp.float32)] + [(shape, jnp.bfloat16)] * (blocks - 1),
        *parts, after=after, moved=16 * blocks * shape[0] * shape[1],
    )


def shards(tokens, q_weight, k_weight, v_weight, d_context):
    head = q_weight.shape[1]
    count, width = tokens.shape
    zs = SIZES[1]
    b16, f32 = jnp.bfloat16, jnp.float32
    product = 64 * count * width * head
    ids = jnp.stack([lax.axis_index(a) for a in AXES]).astype(jnp.int32)

    weights = jnp.concatenate([q_weight, k_weight, v_weight], axis=1)
    inv_wide, normed = call(
        norm_kernel, [((count, 128), f32), ((count, width), b16)], tokens,
        flops=4 * count * width, moved=4 * count * width,
    )
    near = rows(*spread(weights, "zl", RADIX)[::-1], weights, after=(normed,), last_first=True)
    whole = rows(near, *spread(near, "zl", 1))
    w_pieces = (whole, *ring_gather(whole, "x"))
    far = rows(flipped(normed, "zh", 1), after=(whole,), flops=40 * product)
    pair = rows(normed, far, after=w_pieces[1:3])
    t0 = rows(pair, *ring_gather(pair, "y"), after=w_pieces[3:])
    t1 = flipped(t0, "co", 1)

    half = t0.shape[0]
    held = 2 * half
    cosine, sine = (jnp.asarray(t) for t in rope_tables(held, head))
    one_head = ((held, head), b16)
    w_natural, query, kv_mine = call(
        functools.partial(project_kernel, zs),
        [((width, 2 * head), b16), one_head, one_head],
        ids, t0, t1, *w_pieces, cosine, sine,
        flops=product, moved=6 * width * held,
    )
    kv_other = flipped(kv_mine, "co", 1)
    context, d_query, keep, send = call(
        attend_kernel,
        [one_head] * 4,
        ids, query, kv_mine, kv_other, d_context, cosine, sine,
        scratch=[(held, head)] * 2,
        flops=14 * held * held * head, moved=24 * held * head,
    )
    got = flipped(send, "co", 1)
    block = width // SIZES[0]
    p_mine, p_send, joined = call(
        token_grad_kernel,
        [((half, width), b16)] * 2 + [((held, 2 * head), b16)],
        d_query, keep, got, w_natural,
        flops=product, moved=4 * width * held,
    )
    (g_blocks,) = call(
        functools.partial(weight_grad_kernel, zs),
        [((SIZES[0], block, 2 * head), b16)],
        ids, t0, t1, joined,
        scratch=[(block, 2 * head)],
        flops=product, moved=4 * width * held,
    )

    y_own, *y_sent = call(
        part_kernel, [((2 * count, width), f32)] + [((2 * count, width), b16)] * 3, p_mine, flipped(p_send, "co", 1),
        after=(g_blocks,), moved=24 * half * width,
    )
    y_got = [shifted(sent, "y", shift) for sent, shift in zip(y_sent, SHIFTS[1:])]
    kept_t, sent_t = call(
        pair_kernel, [((count, width), f32), ((count, width), b16)], y_own, *y_got, moved=24 * count * width,
    )
    from_zh = flipped(sent_t, "zh", 1)
    (grad_tokens,) = call(
        tokens_out_kernel, [((count, width), b16)], tokens, inv_wide, kept_t, from_zh,
        flops=40 * product, moved=12 * count * width,
    )

    kept, *sent = scatter_sum(RADIX, lax.all_to_all(g_blocks, "x", 0, 0), after=(sent_t,))
    kept, *sent = scatter_sum(RADIX, kept, *collect(sent, "zl", 1))
    cut = kept.shape[0]
    grads = call(
        weights_out_kernel,
        [((cut, head), f32), ((cut, head // 2), f32), ((cut, head // 2), f32)],
        kept, *collect(sent, "zl", RADIX),
        moved=24 * cut * head,
    )
    return (context, grad_tokens, *grads)


def solution(mesh):
    split = P(DP, TENSOR)
    rows = P(DP + TENSOR, None)
    return jax.shard_map(
        shards,
        mesh=Mesh(mesh.devices.reshape(SIZES), AXES),
        in_specs=(rows, split, split, split, split),
        out_specs=(split, rows, split, split, split),
        check_vma=False,
    )
```

```python
import functools
import math

import jax
import jax.numpy as jnp
import numpy as np
from jax import lax
from jax.experimental import pallas as pl
from jax.experimental.pallas import tpu as pltpu
from jax.sharding import Mesh
from jax.sharding import PartitionSpec as P

SEQ = 16
SHIFTS = (0, -1, 1, 2)
VMEM_LIMIT = 20 * 1024 * 1024

AXES = ("x", "za", "zb", "y", "zh", "co")
SIZES = (4, 4, 4, 4, 2, 2)
ZL = ("za", "zb")
DP = ("x", "za", "zb")
TENSOR = ("y", "zh", "co")


def flipped(value, axis, mask):
    size = lax.axis_size(axis)
    return lax.ppermute(value, axis, [(s, s ^ mask) for s in range(size)])


def shifted(value, axis, step):
    size = lax.axis_size(axis)
    return lax.ppermute(value, axis, [(s, (s + step) % size) for s in range(size)])


RADIX = 4


def z_offset(place):
    return place % RADIX * RADIX + place // RADIX


def spread(block, axis, step):
    return tuple(flipped(block, axis, k * step) for k in range(1, RADIX))


def ring_gather(block, axis):
    return tuple(shifted(block, axis, -shift) for shift in SHIFTS[1:])


def added(*terms):
    total = terms[0].astype(jnp.float32)
    for term in terms[1:]:
        total = total + term.astype(jnp.float32)
    return total


def rope_tables(rows, head_size):
    position = (np.arange(rows) % SEQ).astype(np.float32)
    exponent = np.arange(head_size // 2).astype(np.float32) * np.float32(2.0 / head_size)
    inverse = np.exp(-exponent * np.log(np.float32(500000.0)))
    angles = position[:, None] * inverse[None, :]
    cosine, sine = np.cos(angles), np.sin(angles)
    return (
        np.concatenate([cosine, cosine], axis=1).astype(np.float32),
        np.concatenate([-sine, sine], axis=1).astype(np.float32),
    )


def half_roll(value):
    return pltpu.roll(value, value.shape[-1] // 2, 1)


def sequence_at(place, ids):
    co, yq, zh = place // 8, place // 2 % 4, place % 2
    y = (ids[2] + SHIFTS[yq] + 4) % 4
    return y * 4 + (ids[3] ^ zh) * 2 + (ids[4] ^ co)


def norm_kernel(tokens, inv_out, normed_out):
    inputs = tokens[...].astype(jnp.float32)
    inv = lax.rsqrt(jnp.mean(inputs * inputs, axis=-1, keepdims=True) + 1e-05)
    inv_out[...] = jnp.broadcast_to(inv, inv_out.shape)
    normed_out[...] = (inputs * inv).astype(jnp.bfloat16)


def rows_kernel(first, order, *refs):
    *parts, out = refs[first:]
    count = parts[0].shape[0]
    for place, ref in enumerate(parts[::order]):
        out[place * count : (place + 1) * count, :] = ref[...]


def part_kernel(after, mine, got, *outs):
    count = outs[0].shape[0]
    for place, out in enumerate(outs):
        cut = slice(place * count, (place + 1) * count)
        out[...] = added(mine[cut, :], got[cut, :]).astype(out.dtype)


def pair_kernel(own, left, right, far, keep_out, send_out):
    count = keep_out.shape[0]
    for place, out in enumerate((keep_out, send_out)):
        cut = slice(place * count, (place + 1) * count)
        out[...] = added(own[cut, :], left[cut, :], right[cut, :], far[cut, :]).astype(out.dtype)


def scatter_stack_kernel(first, step, *refs):
    ids, stack, out = refs[first:]
    blocks, count = out.shape[:2]
    mine = ids[1] // step % blocks
    for place in range(blocks):
        cut = slice(place * count, (place + 1) * count)
        out[mine ^ place] = added(*(stack[entry, cut, :] for entry in range(stack.shape[0]))).astype(out.dtype)


def weights_out_kernel(parts, q_out, k_out, v_out):
    total = added(*(parts[entry] for entry in range(parts.shape[0])))
    head, half = q_out.shape[1], k_out.shape[1]
    q_out[...] = total[:, :head]
    k_out[...] = total[:, head : head + half]
    v_out[...] = total[:, head + half :]


def tokens_out_kernel(tokens, inv_wide, kept, got, out):
    inputs = tokens[...].astype(jnp.float32)
    d_normed = added(kept[...], got[...])
    inv = inv_wide[:, :1]
    mean = jnp.mean(inputs * d_normed, axis=-1, keepdims=True)
    out[...] = (inv * d_normed - inputs * (inv * inv * inv) * mean).astype(jnp.bfloat16)


def project_kernel(zs, ids, t0, t1, w_own, w_left, w_right, w_far, cos, sin, w_out, q_out, kv_out):
    rows = w_own.shape[0]
    unit = rows // zs
    for ring, ref in enumerate((w_own, w_left, w_right, w_far)):
        block = (ids[0] + SHIFTS[ring] + 4) % 4
        for place in range(zs):
            z = ids[1] ^ z_offset(place)
            at = pl.multiple_of(block * rows + z * unit, unit)
            w_out[pl.ds(at, unit), :] = ref[place * unit : (place + 1) * unit, :]
    totals = []
    for ref in (t0, t1):
        total = None
        for k in range(4):
            cut = slice(k * rows, (k + 1) * rows)
            term = jnp.dot(ref[:, cut], w_out[cut, :], preferred_element_type=jnp.float32)
            total = term if total is None else total + term
        totals.append(total)
    projected = jnp.concatenate(totals, axis=0)
    head = projected.shape[1] // 2
    query = projected[:, :head]
    q_out[...] = (query * cos[...] + half_roll(query) * sin[...]).astype(jnp.bfloat16)
    kv_out[...] = projected[:, head:].astype(jnp.bfloat16)


def attend_kernel(ids, q_ref, mine_ref, other_ref, d_ctx_ref, cos, sin, ctx_out, dq_out, keep_out, send_out, d_ctx, ctx):
    rows, head = q_ref.shape
    half = rows // 2
    scale = 1.0 / math.sqrt(head)
    is_first = ids[4] == 0
    low = lax.broadcasted_iota(jnp.int32, (rows, head), 1) < head // 2
    mine = mine_ref[...].astype(jnp.float32)
    other = jnp.concatenate([other_ref[half:, :], other_ref[:half, :]], axis=0).astype(jnp.float32)
    a = jnp.where(is_first, mine, other)
    b = jnp.where(is_first, other, mine)
    key_raw = jnp.where(low, a, half_roll(b))
    value = jnp.where(low, half_roll(a), b).astype(jnp.bfloat16)
    key = (key_raw * cos[...] + half_roll(key_raw) * sin[...]).astype(jnp.bfloat16)
    query = q_ref[...]
    for place in range(rows // SEQ):
        at = pl.multiple_of(sequence_at(place, ids) * SEQ, SEQ)
        d_ctx[place * SEQ : (place + 1) * SEQ, :] = d_ctx_ref[pl.ds(at, SEQ), :]
    grad_out = d_ctx[...]
    row = lax.broadcasted_iota(jnp.int32, (rows, rows), 0)
    col = lax.broadcasted_iota(jnp.int32, (rows, rows), 1)
    allowed = (row // SEQ == col // SEQ) & (col <= row)
    last = (((1,), (1,)), ((), ()))
    first = (((0,), (0,)), ((), ()))
    dot = functools.partial(lax.dot_general, preferred_element_type=jnp.float32)
    scores = dot(query, key, last) * scale
    masked = jnp.where(allowed, scores, -1e30)
    expd = jnp.exp(masked - jnp.max(masked, axis=-1, keepdims=True))
    probs = expd / jnp.sum(expd, axis=-1, keepdims=True)
    probs_b = probs.astype(jnp.bfloat16)
    ctx[...] = jnp.dot(probs_b, value, preferred_element_type=jnp.float32).astype(jnp.bfloat16)
    for place in range(rows // SEQ):
        at = pl.multiple_of(sequence_at(place, ids) * SEQ, SEQ)
        ctx_out[pl.ds(at, SEQ), :] = ctx[place * SEQ : (place + 1) * SEQ, :]
    d_probs = dot(grad_out, value, last)
    d_scores = probs * (d_probs - jnp.sum(probs * d_probs, axis=-1, keepdims=True)) * scale
    d_scores = d_scores.astype(jnp.bfloat16)
    value_term = dot(probs_b, grad_out, first)
    dq_rot = jnp.dot(d_scores, key, preferred_element_type=jnp.float32)
    dk_rot = dot(d_scores, query, first)
    dq_out[...] = (dq_rot * cos[...] - half_roll(dq_rot) * sin[...]).astype(jnp.bfloat16)
    key_term = dk_rot * cos[...] - half_roll(dk_rot) * sin[...]
    lows = jnp.where(low, key_term, half_roll(value_term))
    highs = jnp.where(low, half_roll(key_term), value_term)
    keep_out[...] = jnp.where(is_first, lows, highs).astype(jnp.bfloat16)
    send_out[...] = jnp.where(is_first, highs, lows).astype(jnp.bfloat16)


def joined_grads(dq_ref, keep_ref, got_ref):
    half = dq_ref.shape[0] // 2
    got = jnp.concatenate([got_ref[half:, :], got_ref[:half, :]], axis=0)
    d_kv = (keep_ref[...].astype(jnp.float32) + got.astype(jnp.float32)).astype(jnp.bfloat16)
    return jnp.concatenate([dq_ref[...], d_kv], axis=1)


def weight_grad_kernel(zs, ids, t0, t1, dj_ref, out, natural):
    half = dj_ref.shape[0] // 2
    blocks, rows = out.shape[:2]
    unit = rows // zs
    dims = (((0,), (0,)), ((), ()))
    for block in range(blocks):
        cut = slice(block * rows, (block + 1) * rows)
        total = lax.dot_general(t0[:, cut], dj_ref[:half, :], dims, preferred_element_type=jnp.float32)
        total += lax.dot_general(t1[:, cut], dj_ref[half:, :], dims, preferred_element_type=jnp.float32)
        natural[...] = total.astype(jnp.bfloat16)
        for place in range(zs):
            at = pl.multiple_of((ids[1] ^ z_offset(place)) * unit, unit)
            out[block, place * unit : (place + 1) * unit, :] = natural[pl.ds(at, unit), :]


def token_grad_kernel(dq_ref, keep_ref, got_ref, w_ref, mine_out, send_out, dj_out):
    dj_out[...] = joined_grads(dq_ref, keep_ref, got_ref)
    half, width = mine_out.shape
    step = width // 4
    dims = (((1,), (1,)), ((), ()))
    for ref, rows in ((send_out, slice(half, None)), (mine_out, slice(0, half))):
        for k in range(4):
            cut = slice(k * step, (k + 1) * step)
            ref[:, cut] = lax.dot_general(
                dj_out[rows, :], w_ref[cut, :], dims, preferred_element_type=jnp.float32
            ).astype(jnp.bfloat16)


def call(kernel, out_shapes, *args, after=(), scratch=(), flops=0, moved=0):
    vmem = pl.BlockSpec(memory_space=pltpu.VMEM)
    smem = pl.BlockSpec(memory_space=pltpu.SMEM)
    in_specs = [smem if a.dtype == jnp.int32 else vmem for a in args]
    in_specs = [pl.BlockSpec(memory_space=pl.ANY)] * len(after) + in_specs
    return pl.pallas_call(
        kernel,
        out_shape=[jax.ShapeDtypeStruct(s, t) for s, t in out_shapes],
        in_specs=in_specs,
        out_specs=[vmem] * len(out_shapes),
        scratch_shapes=[pltpu.VMEM(s, jnp.bfloat16) for s in scratch],
        compiler_params=pltpu.CompilerParams(vmem_limit_bytes=VMEM_LIMIT),
        cost_estimate=pl.CostEstimate(flops=flops, bytes_accessed=moved, transcendentals=0),
    )(*after, *args)


def rows(*parts, after=(), last_first=False, flops=0):
    shape = (len(parts) * parts[0].shape[0], parts[0].shape[1])
    (out,) = call(
        functools.partial(rows_kernel, len(after), -1 if last_first else 1), [(shape, parts[0].dtype)], *parts, after=after,
        flops=flops, moved=4 * shape[0] * shape[1],
    )
    return out


def scatter_stack(ids, step, stack, after=()):
    count = stack.shape[1] // RADIX
    (out,) = call(
        functools.partial(scatter_stack_kernel, len(after), step), [((RADIX, count, stack.shape[2]), jnp.bfloat16)],
        ids, stack, after=after, moved=10 * stack.shape[1] * stack.shape[2],
    )
    return out


def shards(tokens, q_weight, k_weight, v_weight, d_context):
    head = q_weight.shape[1]
    count, width = tokens.shape
    zs = SIZES[1] * SIZES[2]
    b16, f32 = jnp.bfloat16, jnp.float32
    product = 64 * count * width * head
    ids = jnp.stack([lax.axis_index(a) for a in ("x", ZL, "y", "zh", "co")]).astype(jnp.int32)

    weights = jnp.concatenate([q_weight, k_weight, v_weight], axis=1)
    inv_wide, normed = call(
        norm_kernel, [((count, 128), f32), ((count, width), b16)], tokens,
        flops=4 * count * width, moved=4 * count * width,
    )
    near = rows(*spread(weights, ZL, RADIX)[::-1], weights, after=(normed,), last_first=True)
    whole = rows(near, *spread(near, ZL, 1))
    w_pieces = (whole, *ring_gather(whole, "x"))
    far = rows(flipped(normed, "zh", 1), after=(whole,), flops=40 * product)
    pair = rows(normed, far, after=w_pieces[1:3])
    t0 = rows(pair, *ring_gather(pair, "y"), after=w_pieces[3:])
    t1 = flipped(t0, "co", 1)

    half = t0.shape[0]
    held = 2 * half
    cosine, sine = (jnp.asarray(t) for t in rope_tables(held, head))
    one_head = ((held, head), b16)
    w_natural, query, kv_mine = call(
        functools.partial(project_kernel, zs),
        [((width, 2 * head), b16), one_head, one_head],
        ids, t0, t1, *w_pieces, cosine, sine,
        flops=product, moved=6 * width * held,
    )
    kv_other = flipped(kv_mine, "co", 1)
    context, d_query, keep, send = call(
        attend_kernel,
        [one_head] * 4,
        ids, query, kv_mine, kv_other, d_context, cosine, sine,
        scratch=[(held, head)] * 2,
        flops=14 * held * held * head, moved=24 * held * head,
    )
    got = flipped(send, "co", 1)
    block = width // SIZES[0]
    p_mine, p_send, joined = call(
        token_grad_kernel,
        [((half, width), b16)] * 2 + [((held, 2 * head), b16)],
        d_query, keep, got, w_natural,
        flops=product, moved=4 * width * held,
    )
    (g_blocks,) = call(
        functools.partial(weight_grad_kernel, zs),
        [((SIZES[0], block, 2 * head), b16)],
        ids, t0, t1, joined,
        scratch=[(block, 2 * head)],
        flops=product, moved=4 * width * held,
    )

    y_own, *y_sent = call(
        part_kernel, [((2 * count, width), f32)] + [((2 * count, width), b16)] * 3, p_mine, flipped(p_send, "co", 1),
        after=(g_blocks,), moved=24 * half * width,
    )
    y_got = [shifted(sent, "y", shift) for sent, shift in zip(y_sent, SHIFTS[1:])]
    kept_t, sent_t = call(
        pair_kernel, [((count, width), f32), ((count, width), b16)], y_own, *y_got, moved=24 * count * width,
    )
    from_zh = flipped(sent_t, "zh", 1)
    (grad_tokens,) = call(
        tokens_out_kernel, [((count, width), b16)], tokens, inv_wide, kept_t, from_zh,
        flops=40 * product, moved=12 * count * width,
    )

    near = scatter_stack(ids, 1, lax.all_to_all(g_blocks, "x", 0, 0), after=(sent_t,))
    far = scatter_stack(ids, RADIX, lax.all_to_all(near, "zb", 0, 0))
    grads = lax.all_to_all(far, "za", 0, 0)
    cut = grads.shape[1]
    grads = call(
        weights_out_kernel,
        [((cut, head), f32), ((cut, head // 2), f32), ((cut, head // 2), f32)],
        grads,
        moved=24 * cut * head,
    )
    return (context, grad_tokens, *grads)


def solution(mesh):
    split = P(DP, TENSOR)
    rows = P(DP + TENSOR, None)
    return jax.shard_map(
        shards,
        mesh=Mesh(mesh.devices.reshape(SIZES), AXES),
        in_specs=(rows, split, split, split, split),
        out_specs=(split, rows, split, split, split),
        check_vma=False,
    )
```

```python
import functools
import math

import jax
import jax.numpy as jnp
import numpy as np
from jax import lax
from jax.experimental import pallas as pl
from jax.experimental.pallas import tpu as pltpu
from jax.sharding import Mesh
from jax.sharding import PartitionSpec as P

SEQ = 16
SHIFTS = (0, -1, 1, 2)
VMEM_LIMIT = 20 * 1024 * 1024

AXES = ("x", "za", "zb", "y", "zh", "co")
SIZES = (4, 4, 4, 4, 2, 2)
ZL = ("za", "zb")
DP = ("x", "za", "zb")
TENSOR = ("y", "zh", "co")


def flipped(value, axis, mask):
    size = lax.axis_size(axis)
    return lax.ppermute(value, axis, [(s, s ^ mask) for s in range(size)])


def shifted(value, axis, step):
    size = lax.axis_size(axis)
    return lax.ppermute(value, axis, [(s, (s + step) % size) for s in range(size)])


RADIX = 4


def z_offset(place):
    return place % RADIX * RADIX + place // RADIX


def spread(block, axis, step):
    return tuple(flipped(block, axis, k * step) for k in range(1, RADIX))


def ring_gather(block, axis):
    return tuple(shifted(block, axis, -shift) for shift in SHIFTS[1:])


def added(*terms):
    total = terms[0].astype(jnp.float32)
    for term in terms[1:]:
        total = total + term.astype(jnp.float32)
    return total


def rope_tables(rows, head_size):
    position = (np.arange(rows) % SEQ).astype(np.float32)
    exponent = np.arange(head_size // 2).astype(np.float32) * np.float32(2.0 / head_size)
    inverse = np.exp(-exponent * np.log(np.float32(500000.0)))
    angles = position[:, None] * inverse[None, :]
    cosine, sine = np.cos(angles), np.sin(angles)
    return (
        np.concatenate([cosine, cosine], axis=1).astype(np.float32),
        np.concatenate([-sine, sine], axis=1).astype(np.float32),
    )


def half_roll(value):
    return pltpu.roll(value, value.shape[-1] // 2, 1)


def sequence_at(place, ids):
    co, yq, zh = place // 8, place // 2 % 4, place % 2
    y = (ids[2] + SHIFTS[yq] + 4) % 4
    return y * 4 + (ids[3] ^ zh) * 2 + (ids[4] ^ co)


def norm_kernel(ids, tokens, inv_out, normed_out, swap_out):
    inputs = tokens[...].astype(jnp.float32)
    inv = lax.rsqrt(jnp.mean(inputs * inputs, axis=-1, keepdims=True) + 1e-05)
    inv_out[...] = jnp.broadcast_to(inv, inv_out.shape)
    normed_out[...] = (inputs * inv).astype(jnp.bfloat16)
    count = tokens.shape[0]
    swap_out[pl.ds(pl.multiple_of((1 - ids[3]) * count, count), count), :] = normed_out[...]
    swap_out[pl.ds(pl.multiple_of(ids[3] * count, count), count), :] = jnp.zeros_like(normed_out)


def rows_kernel(first, order, *refs):
    *parts, out = refs[first:]
    count = parts[0].shape[0]
    for place, ref in enumerate(parts[::order]):
        out[place * count : (place + 1) * count, :] = ref[...]


def part_kernel(after, mine, got, *outs):
    count = outs[0].shape[0]
    for place, out in enumerate(outs):
        cut = slice(place * count, (place + 1) * count)
        out[...] = added(mine[cut, :], got[cut, :]).astype(out.dtype)


def pair_kernel(ids, own, left, right, far, out):
    count = out.shape[0] // 2
    for place in range(2):
        cut = slice(place * count, (place + 1) * count)
        at = pl.multiple_of((ids[3] ^ place) * count, count)
        out[pl.ds(at, count), :] = added(own[cut, :], left[cut, :], right[cut, :], far[cut, :]).astype(out.dtype)


def scatter_stack_kernel(first, step, *refs):
    ids, stack, out = refs[first:]
    blocks, count = out.shape[:2]
    mine = ids[1] // step % blocks
    for place in range(blocks):
        cut = slice(place * count, (place + 1) * count)
        out[mine ^ place] = added(*(stack[entry, cut, :] for entry in range(stack.shape[0]))).astype(out.dtype)


def weights_out_kernel(parts, q_out, k_out, v_out):
    total = added(*(parts[entry] for entry in range(parts.shape[0])))
    head, half = q_out.shape[1], k_out.shape[1]
    q_out[...] = total[:, :head]
    k_out[...] = total[:, head : head + half]
    v_out[...] = total[:, head + half :]


def tokens_out_kernel(tokens, inv_wide, summed, out):
    inputs = tokens[...].astype(jnp.float32)
    d_normed = summed[...].astype(jnp.float32)
    inv = inv_wide[:, :1]
    mean = jnp.mean(inputs * d_normed, axis=-1, keepdims=True)
    out[...] = (inv * d_normed - inputs * (inv * inv * inv) * mean).astype(jnp.bfloat16)


def project_kernel(zs, ids, t0, t1, w_own, w_left, w_right, w_far, cos, sin, w_out, q_out, kv_out):
    rows = w_own.shape[0]
    unit = rows // zs
    for ring, ref in enumerate((w_own, w_left, w_right, w_far)):
        block = (ids[0] + SHIFTS[ring] + 4) % 4
        for place in range(zs):
            z = ids[1] ^ z_offset(place)
            at = pl.multiple_of(block * rows + z * unit, unit)
            w_out[pl.ds(at, unit), :] = ref[place * unit : (place + 1) * unit, :]
    totals = []
    for ref in (t0, t1):
        total = None
        for k in range(4):
            cut = slice(k * rows, (k + 1) * rows)
            term = jnp.dot(ref[:, cut], w_out[cut, :], preferred_element_type=jnp.float32)
            total = term if total is None else total + term
        totals.append(total)
    projected = jnp.concatenate(totals, axis=0)
    head = projected.shape[1] // 2
    query = projected[:, :head]
    q_out[...] = (query * cos[...] + half_roll(query) * sin[...]).astype(jnp.bfloat16)
    kv_out[...] = projected[:, head:].astype(jnp.bfloat16)


def attend_kernel(ids, q_ref, mine_ref, other_ref, d_ctx_ref, cos, sin, ctx_out, dq_out, keep_out, send_out, d_ctx, ctx):
    rows, head = q_ref.shape
    half = rows // 2
    scale = 1.0 / math.sqrt(head)
    is_first = ids[4] == 0
    low = lax.broadcasted_iota(jnp.int32, (rows, head), 1) < head // 2
    mine = mine_ref[...].astype(jnp.float32)
    other = jnp.concatenate([other_ref[half:, :], other_ref[:half, :]], axis=0).astype(jnp.float32)
    a = jnp.where(is_first, mine, other)
    b = jnp.where(is_first, other, mine)
    key_raw = jnp.where(low, a, half_roll(b))
    value = jnp.where(low, half_roll(a), b).astype(jnp.bfloat16)
    key = (key_raw * cos[...] + half_roll(key_raw) * sin[...]).astype(jnp.bfloat16)
    query = q_ref[...]
    for place in range(rows // SEQ):
        at = pl.multiple_of(sequence_at(place, ids) * SEQ, SEQ)
        d_ctx[place * SEQ : (place + 1) * SEQ, :] = d_ctx_ref[pl.ds(at, SEQ), :]
    grad_out = d_ctx[...]
    row = lax.broadcasted_iota(jnp.int32, (rows, rows), 0)
    col = lax.broadcasted_iota(jnp.int32, (rows, rows), 1)
    allowed = (row // SEQ == col // SEQ) & (col <= row)
    last = (((1,), (1,)), ((), ()))
    first = (((0,), (0,)), ((), ()))
    dot = functools.partial(lax.dot_general, preferred_element_type=jnp.float32)
    scores = dot(query, key, last) * scale
    masked = jnp.where(allowed, scores, -1e30)
    expd = jnp.exp(masked - jnp.max(masked, axis=-1, keepdims=True))
    probs = expd / jnp.sum(expd, axis=-1, keepdims=True)
    probs_b = probs.astype(jnp.bfloat16)
    ctx[...] = jnp.dot(probs_b, value, preferred_element_type=jnp.float32).astype(jnp.bfloat16)
    for place in range(rows // SEQ):
        at = pl.multiple_of(sequence_at(place, ids) * SEQ, SEQ)
        ctx_out[pl.ds(at, SEQ), :] = ctx[place * SEQ : (place + 1) * SEQ, :]
    d_probs = dot(grad_out, value, last)
    d_scores = probs * (d_probs - jnp.sum(probs * d_probs, axis=-1, keepdims=True)) * scale
    d_scores = d_scores.astype(jnp.bfloat16)
    value_term = dot(probs_b, grad_out, first)
    dq_rot = jnp.dot(d_scores, key, preferred_element_type=jnp.float32)
    dk_rot = dot(d_scores, query, first)
    dq_out[...] = (dq_rot * cos[...] - half_roll(dq_rot) * sin[...]).astype(jnp.bfloat16)
    key_term = dk_rot * cos[...] - half_roll(dk_rot) * sin[...]
    lows = jnp.where(low, key_term, half_roll(value_term))
    highs = jnp.where(low, half_roll(key_term), value_term)
    keep_out[...] = jnp.where(is_first, lows, highs).astype(jnp.bfloat16)
    send_out[...] = jnp.where(is_first, highs, lows).astype(jnp.bfloat16)


def joined_grads(dq_ref, keep_ref, got_ref):
    half = dq_ref.shape[0] // 2
    got = jnp.concatenate([got_ref[half:, :], got_ref[:half, :]], axis=0)
    d_kv = (keep_ref[...].astype(jnp.float32) + got.astype(jnp.float32)).astype(jnp.bfloat16)
    return jnp.concatenate([dq_ref[...], d_kv], axis=1)


def weight_grad_kernel(zs, ids, t0, t1, dj_ref, out, natural):
    half = dj_ref.shape[0] // 2
    blocks, rows = out.shape[:2]
    unit = rows // zs
    dims = (((0,), (0,)), ((), ()))
    for block in range(blocks):
        cut = slice(block * rows, (block + 1) * rows)
        total = lax.dot_general(t0[:, cut], dj_ref[:half, :], dims, preferred_element_type=jnp.float32)
        total += lax.dot_general(t1[:, cut], dj_ref[half:, :], dims, preferred_element_type=jnp.float32)
        natural[...] = total.astype(jnp.bfloat16)
        for place in range(zs):
            at = pl.multiple_of((ids[1] ^ z_offset(place)) * unit, unit)
            out[block, place * unit : (place + 1) * unit, :] = natural[pl.ds(at, unit), :]


def token_grad_kernel(dq_ref, keep_ref, got_ref, w_ref, mine_out, send_out, dj_out):
    dj_out[...] = joined_grads(dq_ref, keep_ref, got_ref)
    half, width = mine_out.shape
    step = width // 4
    dims = (((1,), (1,)), ((), ()))
    for ref, rows in ((send_out, slice(half, None)), (mine_out, slice(0, half))):
        for k in range(4):
            cut = slice(k * step, (k + 1) * step)
            ref[:, cut] = lax.dot_general(
                dj_out[rows, :], w_ref[cut, :], dims, preferred_element_type=jnp.float32
            ).astype(jnp.bfloat16)


def call(kernel, out_shapes, *args, after=(), scratch=(), flops=0, moved=0):
    vmem = pl.BlockSpec(memory_space=pltpu.VMEM)
    smem = pl.BlockSpec(memory_space=pltpu.SMEM)
    in_specs = [smem if a.dtype == jnp.int32 else vmem for a in args]
    in_specs = [pl.BlockSpec(memory_space=pl.ANY)] * len(after) + in_specs
    return pl.pallas_call(
        kernel,
        out_shape=[jax.ShapeDtypeStruct(s, t) for s, t in out_shapes],
        in_specs=in_specs,
        out_specs=[vmem] * len(out_shapes),
        scratch_shapes=[pltpu.VMEM(s, jnp.bfloat16) for s in scratch],
        compiler_params=pltpu.CompilerParams(vmem_limit_bytes=VMEM_LIMIT),
        cost_estimate=pl.CostEstimate(flops=flops, bytes_accessed=moved, transcendentals=0),
    )(*after, *args)


def rows(*parts, after=(), last_first=False, flops=0):
    shape = (len(parts) * parts[0].shape[0], parts[0].shape[1])
    (out,) = call(
        functools.partial(rows_kernel, len(after), -1 if last_first else 1), [(shape, parts[0].dtype)], *parts, after=after,
        flops=flops, moved=4 * shape[0] * shape[1],
    )
    return out


def scatter_stack(ids, step, stack, after=()):
    count = stack.shape[1] // RADIX
    (out,) = call(
        functools.partial(scatter_stack_kernel, len(after), step), [((RADIX, count, stack.shape[2]), jnp.bfloat16)],
        ids, stack, after=after, moved=10 * stack.shape[1] * stack.shape[2],
    )
    return out


def shards(tokens, q_weight, k_weight, v_weight, d_context):
    head = q_weight.shape[1]
    count, width = tokens.shape
    zs = SIZES[1] * SIZES[2]
    b16, f32 = jnp.bfloat16, jnp.float32
    product = 64 * count * width * head
    ids = jnp.stack([lax.axis_index(a) for a in ("x", ZL, "y", "zh", "co")]).astype(jnp.int32)

    weights = jnp.concatenate([q_weight, k_weight, v_weight], axis=1)
    inv_wide, normed, swap = call(
        norm_kernel, [((count, 128), f32), ((count, width), b16), ((2 * count, width), b16)], ids, tokens,
        flops=4 * count * width, moved=4 * count * width,
    )
    near = rows(*spread(weights, ZL, RADIX)[::-1], weights, after=(normed,), last_first=True)
    whole = rows(near, *spread(near, ZL, 1))
    w_pieces = (whole, *ring_gather(whole, "x"))
    far = lax.psum_scatter(swap, "zh", scatter_dimension=0, tiled=True)
    pair = rows(normed, far, after=(whole,), flops=40 * product)
    t0 = rows(pair, *ring_gather(pair, "y"), after=w_pieces[1:])
    t1 = flipped(t0, "co", 1)

    half = t0.shape[0]
    held = 2 * half
    cosine, sine = (jnp.asarray(t) for t in rope_tables(held, head))
    one_head = ((held, head), b16)
    w_natural, query, kv_mine = call(
        functools.partial(project_kernel, zs),
        [((width, 2 * head), b16), one_head, one_head],
        ids, t0, t1, *w_pieces, cosine, sine,
        flops=product, moved=6 * width * held,
    )
    kv_other = flipped(kv_mine, "co", 1)
    context, d_query, keep, send = call(
        attend_kernel,
        [one_head] * 4,
        ids, query, kv_mine, kv_other, d_context, cosine, sine,
        scratch=[(held, head)] * 2,
        flops=14 * held * held * head, moved=24 * held * head,
    )
    got = flipped(send, "co", 1)
    block = width // SIZES[0]
    p_mine, p_send, joined = call(
        token_grad_kernel,
        [((half, width), b16)] * 2 + [((held, 2 * head), b16)],
        d_query, keep, got, w_natural,
        flops=product, moved=4 * width * held,
    )
    (g_blocks,) = call(
        functools.partial(weight_grad_kernel, zs),
        [((SIZES[0], block, 2 * head), b16)],
        ids, t0, t1, joined,
        scratch=[(block, 2 * head)],
        flops=product, moved=4 * width * held,
    )

    y_own, *y_sent = call(
        part_kernel, [((2 * count, width), f32)] + [((2 * count, width), b16)] * 3, p_mine, flipped(p_send, "co", 1),
        after=(g_blocks,), moved=24 * half * width,
    )
    y_got = [shifted(sent, "y", shift) for sent, shift in zip(y_sent, SHIFTS[1:])]
    (sent_t,) = call(pair_kernel, [((2 * count, width), b16)], ids, y_own, *y_got, moved=24 * count * width)
    d_normed = lax.psum_scatter(sent_t, "zh", scatter_dimension=0, tiled=True)
    (grad_tokens,) = call(
        tokens_out_kernel, [((count, width), b16)], tokens, inv_wide, d_normed,
        flops=40 * product, moved=12 * count * width,
    )

    near = scatter_stack(ids, 1, lax.all_to_all(g_blocks, "x", 0, 0), after=(sent_t,))
    far = scatter_stack(ids, RADIX, lax.all_to_all(near, "zb", 0, 0))
    grads = lax.all_to_all(far, "za", 0, 0)
    cut = grads.shape[1]
    grads = call(
        weights_out_kernel,
        [((cut, head), f32), ((cut, head // 2), f32), ((cut, head // 2), f32)],
        grads,
        moved=24 * cut * head,
    )
    return (context, grad_tokens, *grads)


def solution(mesh):
    split = P(DP, TENSOR)
    rows = P(DP + TENSOR, None)
    return jax.shard_map(
        shards,
        mesh=Mesh(mesh.devices.reshape(SIZES), AXES),
        in_specs=(rows, split, split, split, split),
        out_specs=(split, rows, split, split, split),
        check_vma=False,
    )
```

```python
import functools
import math

import jax
import jax.numpy as jnp
import numpy as np
from jax import lax
from jax.experimental import pallas as pl
from jax.experimental.pallas import tpu as pltpu
from jax.sharding import Mesh
from jax.sharding import PartitionSpec as P

SEQ = 16
SHIFTS = (0, -1, 1, 2)
VMEM_LIMIT = 20 * 1024 * 1024

AXES = ("x", "za", "zb", "y", "zh", "co")
SIZES = (4, 4, 4, 4, 2, 2)
ZL = ("za", "zb")
DP = ("x", "za", "zb")
TENSOR = ("y", "zh", "co")


def flipped(value, axis, mask):
    size = lax.axis_size(axis)
    return lax.ppermute(value, axis, [(s, s ^ mask) for s in range(size)])


def shifted(value, axis, step):
    size = lax.axis_size(axis)
    return lax.ppermute(value, axis, [(s, (s + step) % size) for s in range(size)])


RADIX = 4


def z_offset(place):
    return place % RADIX * RADIX + place // RADIX


def spread(block, axis, step):
    return tuple(flipped(block, axis, k * step) for k in range(1, RADIX))


def ring_gather(block, axis):
    return tuple(shifted(block, axis, -shift) for shift in SHIFTS[1:])


def added(*terms):
    total = terms[0].astype(jnp.float32)
    for term in terms[1:]:
        total = total + term.astype(jnp.float32)
    return total


def rope_tables(rows, head_size):
    position = (np.arange(rows) % SEQ).astype(np.float32)
    exponent = np.arange(head_size // 2).astype(np.float32) * np.float32(2.0 / head_size)
    inverse = np.exp(-exponent * np.log(np.float32(500000.0)))
    angles = position[:, None] * inverse[None, :]
    cosine, sine = np.cos(angles), np.sin(angles)
    return (
        np.concatenate([cosine, cosine], axis=1).astype(np.float32),
        np.concatenate([-sine, sine], axis=1).astype(np.float32),
    )


def half_roll(value):
    return pltpu.roll(value, value.shape[-1] // 2, 1)


def sequence_at(place, ids):
    co, yq, zh = place // 8, place // 2 % 4, place % 2
    y = (ids[2] + SHIFTS[yq] + 4) % 4
    return y * 4 + (ids[3] ^ zh) * 2 + (ids[4] ^ co)


def norm_kernel(tokens, inv_out, normed_out):
    inputs = tokens[...].astype(jnp.float32)
    inv = lax.rsqrt(jnp.mean(inputs * inputs, axis=-1, keepdims=True) + 1e-05)
    inv_out[...] = jnp.broadcast_to(inv, inv_out.shape)
    normed_out[...] = (inputs * inv).astype(jnp.bfloat16)


def copies_kernel(first, *refs):
    *parts, out = refs[first:]
    count = parts[0].shape[0]
    for place, ref in enumerate(parts[::-1]):
        for entry in range(out.shape[0]):
            out[entry, place * count : (place + 1) * count, :] = ref[...]


def rows_kernel(first, *refs):
    *parts, out = refs[first:]
    count = parts[0].shape[0]
    for place, ref in enumerate(parts):
        out[place * count : (place + 1) * count, :] = ref[...]


def part_kernel(after, mine, got, *outs):
    count = outs[0].shape[0]
    for place, out in enumerate(outs):
        cut = slice(place * count, (place + 1) * count)
        out[...] = added(mine[cut, :], got[cut, :]).astype(out.dtype)


def pair_kernel(own, left, right, far, keep_out, send_out):
    count = keep_out.shape[0]
    for place, out in enumerate((keep_out, send_out)):
        cut = slice(place * count, (place + 1) * count)
        out[...] = added(own[cut, :], left[cut, :], right[cut, :], far[cut, :]).astype(out.dtype)


def scatter_stack_kernel(first, step, *refs):
    ids, stack, out = refs[first:]
    blocks, count = out.shape[:2]
    mine = ids[1] // step % blocks
    for place in range(blocks):
        cut = slice(place * count, (place + 1) * count)
        out[mine ^ place] = added(*(stack[entry, cut, :] for entry in range(stack.shape[0]))).astype(out.dtype)


def weights_out_kernel(parts, q_out, k_out, v_out):
    total = added(*(parts[entry] for entry in range(parts.shape[0])))
    head, half = q_out.shape[1], k_out.shape[1]
    q_out[...] = total[:, :head]
    k_out[...] = total[:, head : head + half]
    v_out[...] = total[:, head + half :]


def tokens_out_kernel(tokens, inv_wide, kept, got, out):
    inputs = tokens[...].astype(jnp.float32)
    d_normed = added(kept[...], got[...])
    inv = inv_wide[:, :1]
    mean = jnp.mean(inputs * d_normed, axis=-1, keepdims=True)
    out[...] = (inv * d_normed - inputs * (inv * inv * inv) * mean).astype(jnp.bfloat16)


def project_kernel(zs, ids, t0, t1, w_all, cos, sin, w_out, q_out, kv_out):
    blocks, rows = w_all.shape[:2]
    unit = rows // zs
    for block in range(blocks):
        for place in range(zs):
            z = (ids[1] // RADIX ^ place % RADIX) * RADIX + place // RADIX
            at = pl.multiple_of(block * rows + z * unit, unit)
            w_out[pl.ds(at, unit), :] = w_all[block, place * unit : (place + 1) * unit, :]
    totals = []
    for ref in (t0, t1):
        total = None
        for k in range(4):
            cut = slice(k * rows, (k + 1) * rows)
            term = jnp.dot(ref[:, cut], w_out[cut, :], preferred_element_type=jnp.float32)
            total = term if total is None else total + term
        totals.append(total)
    projected = jnp.concatenate(totals, axis=0)
    head = projected.shape[1] // 2
    query = projected[:, :head]
    q_out[...] = (query * cos[...] + half_roll(query) * sin[...]).astype(jnp.bfloat16)
    kv_out[...] = projected[:, head:].astype(jnp.bfloat16)


def attend_kernel(ids, q_ref, mine_ref, other_ref, d_ctx_ref, cos, sin, ctx_out, dq_out, keep_out, send_out, d_ctx, ctx):
    rows, head = q_ref.shape
    half = rows // 2
    scale = 1.0 / math.sqrt(head)
    is_first = ids[4] == 0
    low = lax.broadcasted_iota(jnp.int32, (rows, head), 1) < head // 2
    mine = mine_ref[...].astype(jnp.float32)
    other = jnp.concatenate([other_ref[half:, :], other_ref[:half, :]], axis=0).astype(jnp.float32)
    a = jnp.where(is_first, mine, other)
    b = jnp.where(is_first, other, mine)
    key_raw = jnp.where(low, a, half_roll(b))
    value = jnp.where(low, half_roll(a), b).astype(jnp.bfloat16)
    key = (key_raw * cos[...] + half_roll(key_raw) * sin[...]).astype(jnp.bfloat16)
    query = q_ref[...]
    for place in range(rows // SEQ):
        at = pl.multiple_of(sequence_at(place, ids) * SEQ, SEQ)
        d_ctx[place * SEQ : (place + 1) * SEQ, :] = d_ctx_ref[pl.ds(at, SEQ), :]
    grad_out = d_ctx[...]
    row = lax.broadcasted_iota(jnp.int32, (rows, rows), 0)
    col = lax.broadcasted_iota(jnp.int32, (rows, rows), 1)
    allowed = (row // SEQ == col // SEQ) & (col <= row)
    last = (((1,), (1,)), ((), ()))
    first = (((0,), (0,)), ((), ()))
    dot = functools.partial(lax.dot_general, preferred_element_type=jnp.float32)
    scores = dot(query, key, last) * scale
    masked = jnp.where(allowed, scores, -1e30)
    expd = jnp.exp(masked - jnp.max(masked, axis=-1, keepdims=True))
    probs = expd / jnp.sum(expd, axis=-1, keepdims=True)
    probs_b = probs.astype(jnp.bfloat16)
    ctx[...] = jnp.dot(probs_b, value, preferred_element_type=jnp.float32).astype(jnp.bfloat16)
    for place in range(rows // SEQ):
        at = pl.multiple_of(sequence_at(place, ids) * SEQ, SEQ)
        ctx_out[pl.ds(at, SEQ), :] = ctx[place * SEQ : (place + 1) * SEQ, :]
    d_probs = dot(grad_out, value, last)
    d_scores = probs * (d_probs - jnp.sum(probs * d_probs, axis=-1, keepdims=True)) * scale
    d_scores = d_scores.astype(jnp.bfloat16)
    value_term = dot(probs_b, grad_out, first)
    dq_rot = jnp.dot(d_scores, key, preferred_element_type=jnp.float32)
    dk_rot = dot(d_scores, query, first)
    dq_out[...] = (dq_rot * cos[...] - half_roll(dq_rot) * sin[...]).astype(jnp.bfloat16)
    key_term = dk_rot * cos[...] - half_roll(dk_rot) * sin[...]
    lows = jnp.where(low, key_term, half_roll(value_term))
    highs = jnp.where(low, half_roll(key_term), value_term)
    keep_out[...] = jnp.where(is_first, lows, highs).astype(jnp.bfloat16)
    send_out[...] = jnp.where(is_first, highs, lows).astype(jnp.bfloat16)


def joined_grads(dq_ref, keep_ref, got_ref):
    half = dq_ref.shape[0] // 2
    got = jnp.concatenate([got_ref[half:, :], got_ref[:half, :]], axis=0)
    d_kv = (keep_ref[...].astype(jnp.float32) + got.astype(jnp.float32)).astype(jnp.bfloat16)
    return jnp.concatenate([dq_ref[...], d_kv], axis=1)


def weight_grad_kernel(zs, ids, t0, t1, dj_ref, out, natural):
    half = dj_ref.shape[0] // 2
    blocks, rows = out.shape[:2]
    unit = rows // zs
    dims = (((0,), (0,)), ((), ()))
    for block in range(blocks):
        cut = slice(block * rows, (block + 1) * rows)
        total = lax.dot_general(t0[:, cut], dj_ref[:half, :], dims, preferred_element_type=jnp.float32)
        total += lax.dot_general(t1[:, cut], dj_ref[half:, :], dims, preferred_element_type=jnp.float32)
        natural[...] = total.astype(jnp.bfloat16)
        for place in range(zs):
            at = pl.multiple_of((ids[1] ^ z_offset(place)) * unit, unit)
            out[block, place * unit : (place + 1) * unit, :] = natural[pl.ds(at, unit), :]


def token_grad_kernel(dq_ref, keep_ref, got_ref, w_ref, mine_out, send_out, dj_out):
    dj_out[...] = joined_grads(dq_ref, keep_ref, got_ref)
    half, width = mine_out.shape
    step = width // 4
    dims = (((1,), (1,)), ((), ()))
    for ref, rows in ((send_out, slice(half, None)), (mine_out, slice(0, half))):
        for k in range(4):
            cut = slice(k * step, (k + 1) * step)
            ref[:, cut] = lax.dot_general(
                dj_out[rows, :], w_ref[cut, :], dims, preferred_element_type=jnp.float32
            ).astype(jnp.bfloat16)


def call(kernel, out_shapes, *args, after=(), scratch=(), flops=0, moved=0):
    vmem = pl.BlockSpec(memory_space=pltpu.VMEM)
    smem = pl.BlockSpec(memory_space=pltpu.SMEM)
    in_specs = [smem if a.dtype == jnp.int32 else vmem for a in args]
    in_specs = [pl.BlockSpec(memory_space=pl.ANY)] * len(after) + in_specs
    return pl.pallas_call(
        kernel,
        out_shape=[jax.ShapeDtypeStruct(s, t) for s, t in out_shapes],
        in_specs=in_specs,
        out_specs=[vmem] * len(out_shapes),
        scratch_shapes=[pltpu.VMEM(s, jnp.bfloat16) for s in scratch],
        compiler_params=pltpu.CompilerParams(vmem_limit_bytes=VMEM_LIMIT),
        cost_estimate=pl.CostEstimate(flops=flops, bytes_accessed=moved, transcendentals=0),
    )(*after, *args)


def rows(*parts, after=(), flops=0):
    shape = (len(parts) * parts[0].shape[0], parts[0].shape[1])
    (out,) = call(
        functools.partial(rows_kernel, len(after)), [(shape, parts[0].dtype)], *parts, after=after,
        flops=flops, moved=4 * shape[0] * shape[1],
    )
    return out


def copies(entries, *parts, after=()):
    shape = (entries, len(parts) * parts[0].shape[0], parts[0].shape[1])
    (out,) = call(
        functools.partial(copies_kernel, len(after)), [(shape, parts[0].dtype)], *parts, after=after,
        moved=2 * (entries + 1) * shape[1] * shape[2],
    )
    return out


def scatter_stack(ids, step, stack, after=()):
    count = stack.shape[1] // RADIX
    (out,) = call(
        functools.partial(scatter_stack_kernel, len(after), step), [((RADIX, count, stack.shape[2]), jnp.bfloat16)],
        ids, stack, after=after, moved=10 * stack.shape[1] * stack.shape[2],
    )
    return out


def shards(tokens, q_weight, k_weight, v_weight, d_context):
    head = q_weight.shape[1]
    count, width = tokens.shape
    zs = SIZES[1] * SIZES[2]
    b16, f32 = jnp.bfloat16, jnp.float32
    product = 64 * count * width * head
    ids = jnp.stack([lax.axis_index(a) for a in ("x", ZL, "y", "zh", "co")]).astype(jnp.int32)

    weights = jnp.concatenate([q_weight, k_weight, v_weight], axis=1)
    inv_wide, normed = call(
        norm_kernel, [((count, 128), f32), ((count, width), b16)], tokens,
        flops=4 * count * width, moved=4 * count * width,
    )
    near = copies(SIZES[2], *spread(weights, ZL, RADIX)[::-1], weights, after=(normed,))
    near = lax.all_to_all(near, "zb", 0, 0)
    whole = copies(SIZES[0], near.reshape(-1, near.shape[2]))
    far = rows(flipped(normed, "zh", 1), after=(whole,), flops=40 * product)
    pair = rows(normed, far)
    t0 = rows(pair, *ring_gather(pair, "y"))
    w_all = lax.all_to_all(whole, "x", 0, 0)
    t1 = flipped(t0, "co", 1)

    half = t0.shape[0]
    held = 2 * half
    cosine, sine = (jnp.asarray(t) for t in rope_tables(held, head))
    one_head = ((held, head), b16)
    w_natural, query, kv_mine = call(
        functools.partial(project_kernel, zs),
        [((width, 2 * head), b16), one_head, one_head],
        ids, t0, t1, w_all, cosine, sine,
        flops=product, moved=6 * width * held,
    )
    kv_other = flipped(kv_mine, "co", 1)
    context, d_query, keep, send = call(
        attend_kernel,
        [one_head] * 4,
        ids, query, kv_mine, kv_other, d_context, cosine, sine,
        scratch=[(held, head)] * 2,
        flops=14 * held * held * head, moved=24 * held * head,
    )
    got = flipped(send, "co", 1)
    block = width // SIZES[0]
    p_mine, p_send, joined = call(
        token_grad_kernel,
        [((half, width), b16)] * 2 + [((held, 2 * head), b16)],
        d_query, keep, got, w_natural,
        flops=product, moved=4 * width * held,
    )
    (g_blocks,) = call(
        functools.partial(weight_grad_kernel, zs),
        [((SIZES[0], block, 2 * head), b16)],
        ids, t0, t1, joined,
        scratch=[(block, 2 * head)],
        flops=product, moved=4 * width * held,
    )

    y_own, *y_sent = call(
        part_kernel, [((2 * count, width), f32)] + [((2 * count, width), b16)] * 3, p_mine, flipped(p_send, "co", 1),
        after=(g_blocks,), moved=24 * half * width,
    )
    y_got = [shifted(sent, "y", shift) for sent, shift in zip(y_sent, SHIFTS[1:])]
    kept_t, sent_t = call(
        pair_kernel, [((count, width), f32), ((count, width), b16)], y_own, *y_got, moved=24 * count * width,
    )
    from_zh = flipped(sent_t, "zh", 1)
    (grad_tokens,) = call(
        tokens_out_kernel, [((count, width), b16)], tokens, inv_wide, kept_t, from_zh,
        flops=40 * product, moved=12 * count * width,
    )

    near = scatter_stack(ids, 1, lax.all_to_all(g_blocks, "x", 0, 0), after=(sent_t,))
    far = scatter_stack(ids, RADIX, lax.all_to_all(near, "zb", 0, 0))
    grads = lax.all_to_all(far, "za", 0, 0)
    cut = grads.shape[1]
    grads = call(
        weights_out_kernel,
        [((cut, head), f32), ((cut, head // 2), f32), ((cut, head // 2), f32)],
        grads,
        moved=24 * cut * head,
    )
    return (context, grad_tokens, *grads)


def solution(mesh):
    split = P(DP, TENSOR)
    rows = P(DP + TENSOR, None)
    return jax.shard_map(
        shards,
        mesh=Mesh(mesh.devices.reshape(SIZES), AXES),
        in_specs=(rows, split, split, split, split),
        out_specs=(split, rows, split, split, split),
        check_vma=False,
    )
```

```python
import functools
import math

import jax
import jax.numpy as jnp
import numpy as np
from jax import lax
from jax.experimental import pallas as pl
from jax.experimental.pallas import tpu as pltpu
from jax.sharding import Mesh
from jax.sharding import PartitionSpec as P

SEQ = 16
SHIFTS = (0, -1, 1, 2)
VMEM_LIMIT = 20 * 1024 * 1024

AXES = ("x", "za", "zb", "y", "zh", "co")
SIZES = (4, 4, 4, 4, 2, 2)
ZL = ("za", "zb")
DP = ("x", "za", "zb")
TENSOR = ("y", "zh", "co")


def flipped(value, axis, mask):
    size = lax.axis_size(axis)
    return lax.ppermute(value, axis, [(s, s ^ mask) for s in range(size)])


def shifted(value, axis, step):
    size = lax.axis_size(axis)
    return lax.ppermute(value, axis, [(s, (s + step) % size) for s in range(size)])


RADIX = 4


def z_offset(place):
    return place % RADIX * RADIX + place // RADIX


def spread(block, axis, step):
    return tuple(flipped(block, axis, k * step) for k in range(1, RADIX))


def ring_gather(block, axis):
    return tuple(shifted(block, axis, -shift) for shift in SHIFTS[1:])


def added(*terms):
    total = terms[0].astype(jnp.float32)
    for term in terms[1:]:
        total = total + term.astype(jnp.float32)
    return total


def rope_tables(rows, head_size):
    position = (np.arange(rows) % SEQ).astype(np.float32)
    exponent = np.arange(head_size // 2).astype(np.float32) * np.float32(2.0 / head_size)
    inverse = np.exp(-exponent * np.log(np.float32(500000.0)))
    angles = position[:, None] * inverse[None, :]
    cosine, sine = np.cos(angles), np.sin(angles)
    return (
        np.concatenate([cosine, cosine], axis=1).astype(np.float32),
        np.concatenate([-sine, sine], axis=1).astype(np.float32),
    )


def half_roll(value):
    return pltpu.roll(value, value.shape[-1] // 2, 1)


def sequence_at(place, ids):
    co, zh, yq = place // 8, place // 4 % 2, place % 4
    y = (ids[2] + SHIFTS[yq] + 4) % 4
    return y * 4 + (ids[3] ^ zh) * 2 + (ids[4] ^ co)


def norm_kernel(tokens, inv_out, normed_out):
    inputs = tokens[...].astype(jnp.float32)
    inv = lax.rsqrt(jnp.mean(inputs * inputs, axis=-1, keepdims=True) + 1e-05)
    inv_out[...] = jnp.broadcast_to(inv, inv_out.shape)
    normed_out[...] = (inputs * inv).astype(jnp.bfloat16)


def copies_kernel(first, *refs):
    *parts, out = refs[first:]
    count = parts[0].shape[0]
    for place, ref in enumerate(parts[::-1]):
        for entry in range(out.shape[0]):
            out[entry, place * count : (place + 1) * count, :] = ref[...]


def rows_kernel(first, *refs):
    *parts, out = refs[first:]
    count = parts[0].shape[0]
    for place, ref in enumerate(parts):
        out[place * count : (place + 1) * count, :] = ref[...]


def part_kernel(after, mine, got, *outs):
    count = outs[0].shape[0] // 2
    for place, out in enumerate(outs):
        for zh in range(2):
            at = (zh * len(outs) + place) * count
            cut = slice(at, at + count)
            out[zh * count : (zh + 1) * count, :] = added(mine[cut, :], got[cut, :]).astype(out.dtype)


def pair_kernel(own, left, right, far, keep_out, send_out):
    count = keep_out.shape[0]
    for place, out in enumerate((keep_out, send_out)):
        cut = slice(place * count, (place + 1) * count)
        out[...] = added(own[cut, :], left[cut, :], right[cut, :], far[cut, :]).astype(out.dtype)


def scatter_stack_kernel(first, step, *refs):
    ids, stack, out = refs[first:]
    blocks, count = out.shape[:2]
    mine = ids[1] // step % blocks
    for place in range(blocks):
        cut = slice(place * count, (place + 1) * count)
        out[mine ^ place] = added(*(stack[entry, cut, :] for entry in range(stack.shape[0]))).astype(out.dtype)


def weights_out_kernel(parts, q_out, k_out, v_out):
    total = added(*(parts[entry] for entry in range(parts.shape[0])))
    head, half = q_out.shape[1], k_out.shape[1]
    q_out[...] = total[:, :head]
    k_out[...] = total[:, head : head + half]
    v_out[...] = total[:, head + half :]


def tokens_out_kernel(tokens, inv_wide, kept, got, out):
    inputs = tokens[...].astype(jnp.float32)
    d_normed = added(kept[...], got[...])
    inv = inv_wide[:, :1]
    mean = jnp.mean(inputs * d_normed, axis=-1, keepdims=True)
    out[...] = (inv * d_normed - inputs * (inv * inv * inv) * mean).astype(jnp.bfloat16)


def project_kernel(zs, ids, t0, t1, w_all, cos, sin, w_out, q_out, kv_out):
    blocks, rows = w_all.shape[:2]
    unit = rows // zs
    for block in range(blocks):
        for place in range(zs):
            z = (ids[1] // RADIX ^ place % RADIX) * RADIX + place // RADIX
            at = pl.multiple_of(block * rows + z * unit, unit)
            w_out[pl.ds(at, unit), :] = w_all[block, place * unit : (place + 1) * unit, :]
    totals = []
    for ref in (t0, t1):
        total = None
        for k in range(4):
            cut = slice(k * rows, (k + 1) * rows)
            term = jnp.dot(ref[:, cut], w_out[cut, :], preferred_element_type=jnp.float32)
            total = term if total is None else total + term
        totals.append(total)
    projected = jnp.concatenate(totals, axis=0)
    head = projected.shape[1] // 2
    query = projected[:, :head]
    q_out[...] = (query * cos[...] + half_roll(query) * sin[...]).astype(jnp.bfloat16)
    kv_out[...] = projected[:, head:].astype(jnp.bfloat16)


def attend_kernel(ids, q_ref, mine_ref, other_ref, d_ctx_ref, cos, sin, ctx_out, dq_out, keep_out, send_out, d_ctx, ctx):
    rows, head = q_ref.shape
    half = rows // 2
    scale = 1.0 / math.sqrt(head)
    is_first = ids[4] == 0
    low = lax.broadcasted_iota(jnp.int32, (rows, head), 1) < head // 2
    mine = mine_ref[...].astype(jnp.float32)
    other = jnp.concatenate([other_ref[half:, :], other_ref[:half, :]], axis=0).astype(jnp.float32)
    a = jnp.where(is_first, mine, other)
    b = jnp.where(is_first, other, mine)
    key_raw = jnp.where(low, a, half_roll(b))
    value = jnp.where(low, half_roll(a), b).astype(jnp.bfloat16)
    key = (key_raw * cos[...] + half_roll(key_raw) * sin[...]).astype(jnp.bfloat16)
    query = q_ref[...]
    for place in range(rows // SEQ):
        at = pl.multiple_of(sequence_at(place, ids) * SEQ, SEQ)
        d_ctx[place * SEQ : (place + 1) * SEQ, :] = d_ctx_ref[pl.ds(at, SEQ), :]
    grad_out = d_ctx[...]
    row = lax.broadcasted_iota(jnp.int32, (rows, rows), 0)
    col = lax.broadcasted_iota(jnp.int32, (rows, rows), 1)
    allowed = (row // SEQ == col // SEQ) & (col <= row)
    last = (((1,), (1,)), ((), ()))
    first = (((0,), (0,)), ((), ()))
    dot = functools.partial(lax.dot_general, preferred_element_type=jnp.float32)
    scores = dot(query, key, last) * scale
    masked = jnp.where(allowed, scores, -1e30)
    expd = jnp.exp(masked - jnp.max(masked, axis=-1, keepdims=True))
    probs = expd / jnp.sum(expd, axis=-1, keepdims=True)
    probs_b = probs.astype(jnp.bfloat16)
    ctx[...] = jnp.dot(probs_b, value, preferred_element_type=jnp.float32).astype(jnp.bfloat16)
    for place in range(rows // SEQ):
        at = pl.multiple_of(sequence_at(place, ids) * SEQ, SEQ)
        ctx_out[pl.ds(at, SEQ), :] = ctx[place * SEQ : (place + 1) * SEQ, :]
    d_probs = dot(grad_out, value, last)
    d_scores = probs * (d_probs - jnp.sum(probs * d_probs, axis=-1, keepdims=True)) * scale
    d_scores = d_scores.astype(jnp.bfloat16)
    value_term = dot(probs_b, grad_out, first)
    dq_rot = jnp.dot(d_scores, key, preferred_element_type=jnp.float32)
    dk_rot = dot(d_scores, query, first)
    dq_out[...] = (dq_rot * cos[...] - half_roll(dq_rot) * sin[...]).astype(jnp.bfloat16)
    key_term = dk_rot * cos[...] - half_roll(dk_rot) * sin[...]
    lows = jnp.where(low, key_term, half_roll(value_term))
    highs = jnp.where(low, half_roll(key_term), value_term)
    keep_out[...] = jnp.where(is_first, lows, highs).astype(jnp.bfloat16)
    send_out[...] = jnp.where(is_first, highs, lows).astype(jnp.bfloat16)


def joined_grads(dq_ref, keep_ref, got_ref):
    half = dq_ref.shape[0] // 2
    got = jnp.concatenate([got_ref[half:, :], got_ref[:half, :]], axis=0)
    d_kv = (keep_ref[...].astype(jnp.float32) + got.astype(jnp.float32)).astype(jnp.bfloat16)
    return jnp.concatenate([dq_ref[...], d_kv], axis=1)


def weight_grad_kernel(zs, ids, t0, t1, dj_ref, out, natural):
    half = dj_ref.shape[0] // 2
    blocks, rows = out.shape[:2]
    unit = rows // zs
    dims = (((0,), (0,)), ((), ()))
    for block in range(blocks):
        cut = slice(block * rows, (block + 1) * rows)
        total = lax.dot_general(t0[:, cut], dj_ref[:half, :], dims, preferred_element_type=jnp.float32)
        total += lax.dot_general(t1[:, cut], dj_ref[half:, :], dims, preferred_element_type=jnp.float32)
        natural[...] = total.astype(jnp.bfloat16)
        for place in range(zs):
            at = pl.multiple_of((ids[1] ^ z_offset(place)) * unit, unit)
            out[block, place * unit : (place + 1) * unit, :] = natural[pl.ds(at, unit), :]


def token_grad_kernel(dq_ref, keep_ref, got_ref, w_ref, mine_out, send_out, dj_out):
    dj_out[...] = joined_grads(dq_ref, keep_ref, got_ref)
    half, width = mine_out.shape
    step = width // 4
    dims = (((1,), (1,)), ((), ()))
    for ref, rows in ((send_out, slice(half, None)), (mine_out, slice(0, half))):
        for k in range(4):
            cut = slice(k * step, (k + 1) * step)
            ref[:, cut] = lax.dot_general(
                dj_out[rows, :], w_ref[cut, :], dims, preferred_element_type=jnp.float32
            ).astype(jnp.bfloat16)


def call(kernel, out_shapes, *args, after=(), scratch=(), flops=0, moved=0):
    vmem = pl.BlockSpec(memory_space=pltpu.VMEM)
    smem = pl.BlockSpec(memory_space=pltpu.SMEM)
    in_specs = [smem if a.dtype == jnp.int32 else vmem for a in args]
    in_specs = [pl.BlockSpec(memory_space=pl.ANY)] * len(after) + in_specs
    return pl.pallas_call(
        kernel,
        out_shape=[jax.ShapeDtypeStruct(s, t) for s, t in out_shapes],
        in_specs=in_specs,
        out_specs=[vmem] * len(out_shapes),
        scratch_shapes=[pltpu.VMEM(s, jnp.bfloat16) for s in scratch],
        compiler_params=pltpu.CompilerParams(vmem_limit_bytes=VMEM_LIMIT),
        cost_estimate=pl.CostEstimate(flops=flops, bytes_accessed=moved, transcendentals=0),
    )(*after, *args)


def rows(*parts, after=(), flops=0):
    shape = (len(parts) * parts[0].shape[0], parts[0].shape[1])
    (out,) = call(
        functools.partial(rows_kernel, len(after)), [(shape, parts[0].dtype)], *parts, after=after,
        flops=flops, moved=4 * shape[0] * shape[1],
    )
    return out


def copies(entries, *parts, after=()):
    shape = (entries, len(parts) * parts[0].shape[0], parts[0].shape[1])
    (out,) = call(
        functools.partial(copies_kernel, len(after)), [(shape, parts[0].dtype)], *parts, after=after,
        moved=2 * (entries + 1) * shape[1] * shape[2],
    )
    return out


def scatter_stack(ids, step, stack, after=()):
    count = stack.shape[1] // RADIX
    (out,) = call(
        functools.partial(scatter_stack_kernel, len(after), step), [((RADIX, count, stack.shape[2]), jnp.bfloat16)],
        ids, stack, after=after, moved=10 * stack.shape[1] * stack.shape[2],
    )
    return out


def shards(tokens, q_weight, k_weight, v_weight, d_context):
    head = q_weight.shape[1]
    count, width = tokens.shape
    zs = SIZES[1] * SIZES[2]
    b16, f32 = jnp.bfloat16, jnp.float32
    product = 64 * count * width * head
    ids = jnp.stack([lax.axis_index(a) for a in ("x", ZL, "y", "zh", "co")]).astype(jnp.int32)

    weights = jnp.concatenate([q_weight, k_weight, v_weight], axis=1)
    inv_wide, normed = call(
        norm_kernel, [((count, 128), f32), ((count, width), b16)], tokens,
        flops=4 * count * width, moved=4 * count * width,
    )
    near = copies(SIZES[2], *spread(weights, ZL, RADIX)[::-1], weights, after=(normed,))
    near = lax.all_to_all(near, "zb", 0, 0)
    whole = copies(SIZES[0], near.reshape(-1, near.shape[2]))
    own = rows(normed, after=(whole,))
    own_ring = ring_gather(own, "y")
    far = rows(flipped(normed, "zh", 1), after=own_ring, flops=40 * product)
    t0 = rows(own, *own_ring, far, *ring_gather(far, "y"))
    w_all = lax.all_to_all(whole, "x", 0, 0)
    t1 = flipped(t0, "co", 1)

    half = t0.shape[0]
    held = 2 * half
    cosine, sine = (jnp.asarray(t) for t in rope_tables(held, head))
    one_head = ((held, head), b16)
    w_natural, query, kv_mine = call(
        functools.partial(project_kernel, zs),
        [((width, 2 * head), b16), one_head, one_head],
        ids, t0, t1, w_all, cosine, sine,
        flops=product, moved=6 * width * held,
    )
    kv_other = flipped(kv_mine, "co", 1)
    context, d_query, keep, send = call(
        attend_kernel,
        [one_head] * 4,
        ids, query, kv_mine, kv_other, d_context, cosine, sine,
        scratch=[(held, head)] * 2,
        flops=14 * held * held * head, moved=24 * held * head,
    )
    got = flipped(send, "co", 1)
    block = width // SIZES[0]
    p_mine, p_send, joined = call(
        token_grad_kernel,
        [((half, width), b16)] * 2 + [((held, 2 * head), b16)],
        d_query, keep, got, w_natural,
        flops=product, moved=4 * width * held,
    )
    (g_blocks,) = call(
        functools.partial(weight_grad_kernel, zs),
        [((SIZES[0], block, 2 * head), b16)],
        ids, t0, t1, joined,
        scratch=[(block, 2 * head)],
        flops=product, moved=4 * width * held,
    )

    y_own, *y_sent = call(
        part_kernel, [((2 * count, width), f32)] + [((2 * count, width), b16)] * 3, p_mine, flipped(p_send, "co", 1),
        after=(g_blocks,), moved=24 * half * width,
    )
    y_got = [shifted(sent, "y", shift) for sent, shift in zip(y_sent, SHIFTS[1:])]
    kept_t, sent_t = call(
        pair_kernel, [((count, width), f32), ((count, width), b16)], y_own, *y_got, moved=24 * count * width,
    )
    from_zh = flipped(sent_t, "zh", 1)
    (grad_tokens,) = call(
        tokens_out_kernel, [((count, width), b16)], tokens, inv_wide, kept_t, from_zh,
        flops=40 * product, moved=12 * count * width,
    )

    near = scatter_stack(ids, 1, lax.all_to_all(g_blocks, "x", 0, 0), after=(sent_t,))
    far = scatter_stack(ids, RADIX, lax.all_to_all(near, "zb", 0, 0))
    grads = lax.all_to_all(far, "za", 0, 0)
    cut = grads.shape[1]
    grads = call(
        weights_out_kernel,
        [((cut, head), f32), ((cut, head // 2), f32), ((cut, head // 2), f32)],
        grads,
        moved=24 * cut * head,
    )
    return (context, grad_tokens, *grads)


def solution(mesh):
    split = P(DP, TENSOR)
    rows = P(DP + TENSOR, None)
    return jax.shard_map(
        shards,
        mesh=Mesh(mesh.devices.reshape(SIZES), AXES),
        in_specs=(rows, split, split, split, split),
        out_specs=(split, rows, split, split, split),
        check_vma=False,
    )
```
